256 devices in a mesh: row: 32 (over z, y), col: 8 (over x, core).
Axes of the slice: x: 4, y: 4, z: 8, core: 2. Of those that a mesh axis runs over, the one named last changes fastest.
Arguments:
- image: bfloat16 [16384, 512], P(('row', 'col')), may hold values from -2 to 2
- text: bfloat16 [16384, 512], P(('row', 'col')), may hold values from -3 to 3
- logit_scale: float32 [1], replicated, may hold values from 10 to 100
Outputs:
- loss: float32 [1], replicated
- grad_image: float32 [16384, 512], P(('row', 'col'))
- grad_text: float32 [16384, 512], P(('row', 'col'))
The draws below stay inside these ranges and needn't reach their ends.
All inputs are finite; a program needn't handle non-finite values.
Results may differ from the reference program's by a relative error of at most 0.0095.
Values may be sent and summed in bfloat16 or wider, within the bound.
A program may use at most 64 MiB of HBM per device.

```python
import jax
import jax.numpy as jnp
from jax import lax

E = 512
BATCH = 16384


def embed_pair(key):
    keys = jax.random.split(jax.random.fold_in(key, 11), 4)
    position = jnp.arange(BATCH)
    fraction = (position.astype(jnp.float32) / BATCH)[:, None]
    img_raw = jax.random.normal(keys[0], (BATCH, E), jnp.float32)
    agreement = 1.6 * (1.0 - fraction)
    noise = jax.random.normal(keys[1], (BATCH, E), jnp.float32)
    txt_raw = agreement * img_raw + noise
    img_scale = jnp.exp(jax.random.uniform(keys[2], (BATCH, 1), jnp.float32, -0.69, 0.69))
    txt_scale = jnp.exp(jax.random.uniform(keys[3], (BATCH, 1), jnp.float32, -0.69, 0.69))
    img_out = jnp.clip(img_raw * img_scale * 0.25, -2.0, 2.0)
    txt_out = jnp.clip(txt_raw * txt_scale * 0.25, -3.0, 3.0)
    return (img_out, txt_out)


def draw_image(key, part):
    return embed_pair(key)[0].astype(jnp.bfloat16)


def draw_text(key, part):
    return embed_pair(key)[1].astype(jnp.bfloat16)


def draw_logit_scale(key, part):
    return jax.random.uniform(jax.random.fold_in(key, 23), (1,), jnp.float32, 10.0, 30.0)


def setup_inputs(seed: int = 0) -> dict:
    key_list = jax.random.split(jax.random.key(seed), 4)
    return {
        "image": draw_image(jax.random.fold_in(key_list[3], 71), 0),
        "text": draw_text(jax.random.fold_in(key_list[3], 71), 0),
        "logit_scale": draw_logit_scale(jax.random.fold_in(key_list[3], 71), 0),
    }


def normalize(embedding):
    values = embedding.astype(jnp.float32)
    length = jnp.sqrt(lax.optimization_barrier(jnp.sum(values * values, axis=1, keepdims=True)) + 1e-06)
    return (values / length, length)

def unnormalize(unit_rows, length, gradient):
    return (gradient - unit_rows * lax.optimization_barrier(jnp.sum(unit_rows * gradient, axis=1, keepdims=True))) / length

def reference(image, text, logit_scale):
    sharpness = logit_scale[0]
    unit_image, image_len = normalize(image)
    unit_text, text_len = normalize(text)
    img_half = unit_image.astype(jnp.bfloat16)
    txt_half = unit_text.astype(jnp.bfloat16)
    block_rows = min(1024, BATCH)
    block_count = BATCH // block_rows
    img_blocks = img_half.reshape(block_count, block_rows, E)

    def stats(running, img_block):
        col_peak, col_sum = running
        logits = sharpness * jnp.dot(img_block, txt_half.T, preferred_element_type=jnp.float32)
        row_peak = lax.optimization_barrier(jnp.max(logits, axis=1))
        row_lse = row_peak + jnp.log(lax.optimization_barrier(jnp.sum(jnp.exp(logits - row_peak[:, None]), axis=1)))
        higher = jnp.maximum(col_peak, lax.optimization_barrier(jnp.max(logits, axis=0)))
        col_sum = col_sum * jnp.exp(col_peak - higher) + lax.optimization_barrier(jnp.sum(jnp.exp(logits - higher[None, :]), axis=0))
        return ((higher, col_sum), row_lse)
    lowest = jnp.full((BATCH,), -1e+30, jnp.float32)
    (col_peak, col_sum), row_lse = lax.scan(stats, (lowest, jnp.zeros((BATCH,), jnp.float32)), img_blocks)
    row_lse = row_lse.reshape(BATCH)
    col_lse = col_peak + jnp.log(col_sum)
    positive = sharpness * lax.optimization_barrier(jnp.sum(img_half.astype(jnp.float32) * txt_half.astype(jnp.float32), axis=1))
    loss = ((jnp.sum(row_lse - positive) + jnp.sum(col_lse - positive)) / (2 * BATCH)).reshape(1)

    def backward(running, inputs):
        img_block, lse_rows = inputs
        logits = sharpness * jnp.dot(img_block, txt_half.T, preferred_element_type=jnp.float32)
        weights = (0.5 * (jnp.exp(logits - lse_rows[:, None]) + jnp.exp(logits - col_lse[None, :]))).astype(jnp.bfloat16)
        img_grad = sharpness * jnp.dot(weights, txt_half, preferred_element_type=jnp.float32)
        running = running + sharpness * jnp.dot(weights.T, img_block, preferred_element_type=jnp.float32)
        return (running, img_grad)
    txt_grad, img_grad = lax.scan(backward, jnp.zeros((BATCH, E), jnp.float32), (img_blocks, row_lse.reshape(block_count, block_rows)))
    img_grad = img_grad.reshape(BATCH, E) - sharpness * txt_half.astype(jnp.float32)
    txt_grad = txt_grad - sharpness * img_half.astype(jnp.float32)
    return (loss, unnormalize(unit_image, image_len, img_grad), unnormalize(unit_text, text_len, txt_grad))
```

```python
import functools
import math

import jax
import jax.numpy as jnp
from jax import lax
from jax.experimental import pallas as pl
from jax.experimental.pallas import tpu as pltpu
from jax.sharding import Mesh
from jax.sharding import PartitionSpec as P

MESH = pl.DeviceIdType.MESH
AXES = ("z", "y", "x", "core")
SIZE = {"z": 8, "y": 4, "x": 4, "core": 2}
NT = (((1,), (1,)), ((), ()))
TN = (((0,), (0,)), ((), ()))
NN = (((1,), (0,)), ((), ()))

LINE = [(k, d) for k in range(2) for d in range(8)]
PLANE = [(dy, dx) for dy in range(4) for dx in range(4)]


def at_line(k, d):
    return {
        "z": lax.rem(lax.axis_index("z") + d, 8),
        "core": lax.rem(lax.axis_index("core") + k, 2),
    }


def at_plane(dy, dx):
    return {
        "y": lax.rem(lax.axis_index("y") + dy, 4),
        "x": lax.rem(lax.axis_index("x") + dx, 4),
    }


def back_line(k, d):
    return k * 8 + (8 - d) % 8


def back_plane(dy, dx):
    return ((4 - dy) % 4) * 4 + (4 - dx) % 4


def kernel(
    batch, image_ref, text_ref, scale_ref, loss_ref, img_grad_ref, txt_grad_ref,
    img, txt, half, weights, row_part, row_scale, col_hi, col_lo,
    row_stat, col_stat, row_loss, col_loss,
    img_out, img_pair, txt_out, img_in, txt_in, img_own, txt_own,
    img_s, img_r, pair_s, pair_r, txt_s, txt_r,
    rstat_s, rstat_r, cstat_s, cstat_r, rloss_s, rloss_r, closs_s, closs_r,
    pg_s, pg_r, ig_s, ig_r, tg_s, tg_r,
):
    n = 64
    scale = scale_ref[0]

    def copy(src, dst, s, r, to):
        return pltpu.make_async_remote_copy(
            src_ref=src, dst_ref=dst, send_sem=s, recv_sem=r, device_id=to, device_id_type=MESH
        )

    barrier = pltpu.get_barrier_semaphore()
    for k, d in LINE[1:]:
        pl.semaphore_signal(barrier, inc=1, device_id=at_line(k, d), device_id_type=MESH)
    for dy, dx in PLANE[1:]:
        pl.semaphore_signal(barrier, inc=1, device_id=at_plane(dy, dx), device_id_type=MESH)

    def normal(ref):
        wide = ref[...].astype(jnp.float32)
        length = jnp.sqrt(jnp.sum(wide * wide, axis=1, keepdims=True) + 1e-6)
        return wide / length, length

    unit_image, image_len = normal(image_ref)
    unit_text, text_len = normal(text_ref)
    img[0] = unit_image.astype(jnp.bfloat16)
    txt[0] = unit_text.astype(jnp.bfloat16)
    pl.semaphore_wait(barrier, 30)

    sends = []
    for dy, dx in PLANE[1:]:
        b = back_plane(dy, dx)
        c = copy(txt.at[0], txt.at[b], txt_s.at[b], txt_r.at[b], at_plane(dy, dx))
        c.start()
        sends.append(c)
    for d in (4, 3, 5, 2, 6, 1, 7):
        b = back_line(0, d)
        c = copy(img.at[0], img.at[b], img_s.at[b], img_r.at[b], at_line(0, d))
        c.start()
        sends.append(c)
    pairs = []
    for d in (0, 1, 7, 2, 6, 3, 5, 4):
        if d:
            copy(img.at[d], img.at[d], img_s.at[d], img_r.at[d], at_line(0, 0)).wait_recv()
        c = copy(img.at[d], img.at[8 + d], pair_s.at[d], pair_r.at[d], at_line(1, 0))
        c.start()
        pairs.append(c)
    for d in range(8):
        pairs[d].wait_recv()
    for j in range(1, 16):
        copy(txt.at[j], txt.at[j], txt_s.at[j], txt_r.at[j], at_plane(0, 0)).wait_recv()

    power = scale * (0.5 * math.log2(math.e))
    down, up = math.exp(-15.0), math.exp(15.0)
    col_hi[...] = jnp.zeros_like(col_hi)
    col_lo[...] = jnp.zeros_like(col_lo)

    def strip(i, carry):
        r = pl.multiple_of(i * 128, 128)
        rows = img[pl.ds(2 * i, 2)].reshape(128, 512)
        hi_row = jnp.zeros((128, 128), jnp.float32)
        lo_row = jnp.zeros((128, 128), jnp.float32)
        for q in range(4):
            cols = txt[q * 4 : q * 4 + 4].reshape(256, 512)
            dots = lax.dot_general(rows, cols, NT, preferred_element_type=jnp.float32)
            f = jnp.exp2(dots * power)
            half[pl.ds(r, 128), q * 256 : q * 256 + 256] = f
            hi = f * down
            hi = hi * hi
            lo = jnp.minimum(f, 1.0) * up
            lo = lo * lo
            hi_row = hi_row + (hi[:, :128] + hi[:, 128:])
            lo_row = lo_row + (lo[:, :128] + lo[:, 128:])
            col_hi[:, q * 256 : q * 256 + 256] += jnp.sum(hi.reshape(16, 8, 256), axis=0)
            col_lo[:, q * 256 : q * 256 + 256] += jnp.sum(lo.reshape(16, 8, 256), axis=0)
        row_part[0, pl.ds(r, 128), :] = hi_row
        row_part[1, pl.ds(r, 128), :] = lo_row
        return carry

    lax.fori_loop(0, 8, strip, 0)

    def log_of(hi, lo):
        return jnp.where(
            hi >= math.exp(-30.0), jnp.log(hi) + 30.0, jnp.log(lo) - 30.0
        )

    row_hi = jnp.sum(row_part[0].T, axis=0, keepdims=True)
    row_lo = jnp.sum(row_part[1].T, axis=0, keepdims=True)
    row_stat[0, :, :1024] = log_of(row_hi, row_lo)
    same = img[0].astype(jnp.float32) * txt[0].astype(jnp.float32)
    positive = scale * jnp.sum(same)
    row_stat[0, :, 1024:] = jnp.full((1, 128), positive, jnp.float32)
    for k, d in LINE[1:]:
        b = back_line(k, d)
        c = copy(row_stat.at[0], row_stat.at[b], rstat_s.at[b], rstat_r.at[b], at_line(k, d))
        c.start()
        sends.append(c)
    col_stat[0] = log_of(
        jnp.sum(col_hi[...], axis=0, keepdims=True), jnp.sum(col_lo[...], axis=0, keepdims=True)
    )
    for dy, dx in PLANE[1:]:
        b = back_plane(dy, dx)
        c = copy(col_stat.at[0], col_stat.at[b], cstat_s.at[b], cstat_r.at[b], at_plane(dy, dx))
        c.start()
        sends.append(c)
    for j in range(1, 16):
        copy(row_stat.at[j], row_stat.at[j], rstat_s.at[j], rstat_r.at[j], at_line(0, 0)).wait_recv()
    for j in range(1, 16):
        copy(col_stat.at[j], col_stat.at[j], cstat_s.at[j], cstat_r.at[j], at_plane(0, 0)).wait_recv()

    def row_order(j):
        k, d = j // 8, j % 8
        parts = row_stat[j, :, :1024]
        pieces = [None] * 16
        for k2, d2 in LINE:
            here = ((k + k2) % 2) * 8 + (d + d2) % 8
            there = k2 * 8 + d2
            pieces[here] = parts[:, there * n : there * n + n]
        return jnp.concatenate(pieces, axis=1)

    def col_order(j):
        y0, x0 = j // 4, j % 4
        parts = col_stat[j]
        pieces = [None] * 16
        for y2, x2 in PLANE:
            here = ((y0 + y2) % 4) * 4 + (x0 + x2) % 4
            there = y2 * 4 + x2
            pieces[here] = parts[:, there * n : there * n + n]
        return jnp.concatenate(pieces, axis=1)

    def merged(parts):
        summit = functools.reduce(jnp.maximum, parts)
        total = sum(jnp.exp(p - summit) for p in parts)
        return summit + jnp.log(total)

    row_lse = merged([row_order(j) for j in range(16)])
    col_lse = merged([col_order(j) for j in range(16)])
    all_positive = sum(row_stat[j, :, 1024:] for j in range(16))
    row_loss[0] = jnp.full((1, 128), jnp.sum(row_lse), jnp.float32) - 2.0 * all_positive
    col_loss[0] = jnp.full((1, 128), jnp.sum(col_lse), jnp.float32)
    for dy, dx in PLANE[1:]:
        b = back_plane(dy, dx)
        c = copy(row_loss.at[0], row_loss.at[b], rloss_s.at[b], rloss_r.at[b], at_plane(dy, dx))
        c.start()
        sends.append(c)
    for k, d in LINE[1:]:
        b = back_line(k, d)
        c = copy(col_loss.at[0], col_loss.at[b], closs_s.at[b], closs_r.at[b], at_line(k, d))
        c.start()
        sends.append(c)

    root = math.sqrt(0.5)
    row_factor = jnp.exp(row_lse * -0.5) * root
    col_factor = jnp.exp(col_lse * -0.5) * root
    row_scale[...] = jnp.broadcast_to(row_factor, (128, 1024)).T

    def weigh(i, carry):
        r = pl.multiple_of(i * 64, 64)
        a = row_scale[pl.ds(r, 64), :]
        for q in range(8):
            f = half[pl.ds(r, 64), q * 128 : q * 128 + 128]
            by_row = f * a
            by_col = f * col_factor[:, q * 128 : q * 128 + 128]
            weights[pl.ds(r, 64), q * 128 : q * 128 + 128] = (
                by_row * by_row + by_col * by_col
            ).astype(jnp.bfloat16)
        return carry

    lax.fori_loop(0, 16, weigh, 0)

    texts = txt[...].reshape(1024, 512)
    images = img[...].reshape(1024, 512)
    pair_sends = []
    for h in range(2):
        part = jnp.dot(
            weights[512 + h * 256 : 768 + h * 256, :], texts, preferred_element_type=jnp.float32
        )
        img_out[1, 4 * h : 4 * h + 4] = part.astype(jnp.bfloat16).reshape(4, 64, 512)
        c = copy(
            img_out.at[1, pl.ds(4 * h, 4)], img_pair.at[pl.ds(4 * h, 4)],
            pg_s.at[h], pg_r.at[h], at_line(1, 0),
        )
        c.start()
        pair_sends.append(c)
    for h in range(4):
        part = lax.dot_general(
            weights[:, h * 256 : h * 256 + 256], images, TN, preferred_element_type=jnp.float32
        )
        if h == 0:
            txt_own[...] = part[:64]
        txt_out[4 * h : 4 * h + 4] = part.astype(jnp.bfloat16).reshape(4, 64, 512)
        for j in range(4 * h, 4 * h + 4):
            if j:
                dy, dx = PLANE[j]
                b = back_plane(dy, dx)
                c = copy(txt_out.at[j], txt_in.at[b], tg_s.at[b], tg_r.at[b], at_plane(dy, dx))
                c.start()
                sends.append(c)
    for h in (1, 0):
        part = jnp.dot(weights[h * 256 : h * 256 + 256, :], texts, preferred_element_type=jnp.float32)
        pair_sends[h].wait_recv()
        part = part + img_pair[4 * h : 4 * h + 4].astype(jnp.float32).reshape(256, 512)
        if h == 0:
            img_own[...] = part[:64]
        img_out[0, 4 * h : 4 * h + 4] = part.astype(jnp.bfloat16).reshape(4, 64, 512)
        for d in range(4 * h, 4 * h + 4):
            if d:
                b = back_line(0, d)
                c = copy(img_out.at[0, d], img_in.at[b], ig_s.at[b], ig_r.at[b], at_line(0, d))
                c.start()
                sends.append(c)

    def finish(own, parts, other, unit, length):
        total = own[...]
        for part in parts:
            total = total + part.astype(jnp.float32)
        gradient = scale * total - scale * other.astype(jnp.float32)
        return (gradient - unit * jnp.sum(unit * gradient, axis=1, keepdims=True)) / length

    for d in range(1, 8):
        copy(img_in.at[d], img_in.at[d], ig_s.at[d], ig_r.at[d], at_line(0, 0)).wait_recv()
    img_grad_ref[...] = finish(
        img_own, [img_in[d] for d in range(1, 8)], txt[0], unit_image, image_len
    )
    for j in range(1, 16):
        copy(txt_in.at[j], txt_in.at[j], tg_s.at[j], tg_r.at[j], at_plane(0, 0)).wait_recv()
    txt_grad_ref[...] = finish(
        txt_own, [txt_in[j] for j in range(1, 16)], img[0], unit_text, text_len
    )
    for j in range(1, 16):
        copy(row_loss.at[j], row_loss.at[j], rloss_s.at[j], rloss_r.at[j], at_line(0, 0)).wait_recv()
        copy(col_loss.at[j], col_loss.at[j], closs_s.at[j], closs_r.at[j], at_line(0, 0)).wait_recv()
    total = sum(row_loss[j] + col_loss[j] for j in range(16))
    loss_ref[...] = total / (2.0 * batch)
    for c in sends + pairs + pair_sends:
        c.wait_send()


def on_device(image, text, logit_scale):
    batch = image.shape[0] * 256
    f32, bf16 = jnp.float32, jnp.bfloat16
    dma = pltpu.SemaphoreType.DMA
    vmem = pltpu.VMEM
    loss, img_grad, txt_grad = pl.pallas_call(
        functools.partial(kernel, batch),
        out_shape=(
            jax.ShapeDtypeStruct((1, 128), f32),
            jax.ShapeDtypeStruct((64, 512), f32),
            jax.ShapeDtypeStruct((64, 512), f32),
        ),
        in_specs=[
            pl.BlockSpec(memory_space=vmem),
            pl.BlockSpec(memory_space=vmem),
            pl.BlockSpec(memory_space=pltpu.SMEM),
        ],
        out_specs=[pl.BlockSpec(memory_space=vmem)] * 3,
        scratch_shapes=[
            vmem((16, 64, 512), bf16),
            vmem((16, 64, 512), bf16),
            vmem((1024, 1024), f32),
            vmem((1024, 1024), bf16),
            vmem((2, 1024, 128), f32),
            vmem((1024, 128), f32),
            vmem((8, 1024), f32),
            vmem((8, 1024), f32),
            vmem((16, 1, 1152), f32),
            vmem((16, 1, 1024), f32),
            vmem((16, 1, 128), f32),
            vmem((16, 1, 128), f32),
            vmem((2, 8, 64, 512), bf16),
            vmem((8, 64, 512), bf16),
            vmem((16, 64, 512), bf16),
            vmem((8, 64, 512), bf16),
            vmem((16, 64, 512), bf16),
            vmem((64, 512), f32),
            vmem((64, 512), f32),
            dma((8,)), dma((8,)), dma((8,)), dma((8,)), dma((16,)), dma((16,)),
            dma((16,)), dma((16,)), dma((16,)), dma((16,)), dma((16,)), dma((16,)), dma((16,)), dma((16,)),
            dma((2,)), dma((2,)), dma((8,)), dma((8,)), dma((16,)), dma((16,)),
        ],
        compiler_params=pltpu.CompilerParams(
            collective_id=0, has_side_effects=True, vmem_limit_bytes=56 * 2**20
        ),
        cost_estimate=pl.CostEstimate(
            flops=6 * 1024 * 1024 * 512, bytes_accessed=400000, transcendentals=1024 * 1024
        ),
        name="contrast",
    )(image, text, logit_scale)
    return loss[0, :1], img_grad, txt_grad


def solution(mesh):
    torus = Mesh(mesh.devices.reshape(8, 4, 4, 2), AXES)
    return jax.shard_map(
        on_device,
        mesh=torus,
        in_specs=(P(AXES, None), P(AXES, None), P()),
        out_specs=(P(), P(AXES, None), P(AXES, None)),
        check_vma=False,
    )
```

```python
import functools
import math

import jax
import jax.numpy as jnp
from jax import lax
from jax.experimental import pallas as pl
from jax.experimental.pallas import tpu as pltpu
from jax.sharding import Mesh
from jax.sharding import PartitionSpec as P

MESH = pl.DeviceIdType.MESH
AXES = ("z", "y", "x", "core")
SIZE = {"z": 8, "y": 4, "x": 4, "core": 2}
NT = (((1,), (1,)), ((), ()))
TN = (((0,), (0,)), ((), ()))
NN = (((1,), (0,)), ((), ()))

NEAR = [0, 2, 6, 1, 7]
FAR = [3, 5, 4]
LINE = [(0, d) for d in NEAR] + [(1, d) for d in NEAR] + [(0, d) for d in FAR] + [(1, d) for d in FAR]
PLANE = [
    (0, 0), (0, 1), (0, 3), (1, 0), (3, 0), (0, 2), (2, 0), (1, 1),
    (1, 3), (3, 1), (3, 3), (1, 2), (3, 2), (2, 1), (2, 3), (2, 2),
]
ISLOT = {p: j for j, p in enumerate(LINE)}
TSLOT = {p: j for j, p in enumerate(PLANE)}
ROUND = (2, 1, 3)


def at_line(k, d):
    return {
        "z": lax.rem(lax.axis_index("z") + d, 8),
        "core": lax.rem(lax.axis_index("core") + k, 2),
    }


def at_plane(dy, dx):
    return {
        "y": lax.rem(lax.axis_index("y") + dy, 4),
        "x": lax.rem(lax.axis_index("x") + dx, 4),
    }


def kernel(
    batch, image_ref, text_ref, scale_ref, loss_ref, img_grad_ref, txt_grad_ref,
    raw_img, raw_txt, raw_scale, img, txt, half, weights, row_part, row_scale, col_hi, col_lo,
    row_stat, col_stat, row_loss, col_loss,
    img_out, img_pair, img_hold, img_mid, img_send, img_in, img_own,
    txt_out, txt_mid, txt_send, txt_in,
    load, txt_s, txt_r, img_s, img_r, pair_s, pair_r,
    rstat_s, rstat_r, cstat_s, cstat_r, rloss_s, rloss_r, closs_s, closs_r,
    pg_s, pg_r, im_s, im_r, ig_s, ig_r, tm_s, tm_r, tg_s, tg_r,
):
    n = 64
    f32, bf16 = jnp.float32, jnp.bfloat16

    def copy(src, dst, s, r, to):
        return pltpu.make_async_remote_copy(
            src_ref=src, dst_ref=dst, send_sem=s, recv_sem=r, device_id=to, device_id_type=MESH
        )

    barrier = pltpu.get_barrier_semaphore()
    for k, d in LINE[1:]:
        pl.semaphore_signal(barrier, inc=1, device_id=at_line(k, d), device_id_type=MESH)
    for dy, dx in PLANE[1:]:
        pl.semaphore_signal(barrier, inc=1, device_id=at_plane(dy, dx), device_id_type=MESH)
    loads = [
        pltpu.make_async_copy(image_ref, raw_img, load.at[0]),
        pltpu.make_async_copy(text_ref, raw_txt, load.at[1]),
        pltpu.make_async_copy(scale_ref, raw_scale, load.at[2]),
    ]
    for c in loads:
        c.start()
    col_hi[...] = jnp.zeros_like(col_hi)
    col_lo[...] = jnp.zeros_like(col_lo)
    row_part[...] = jnp.zeros_like(row_part)
    for c in loads:
        c.wait()
    scale = raw_scale[0]

    def normal(ref):
        wide = ref[...].astype(f32)
        length = jnp.sqrt(jnp.sum(wide * wide, axis=1, keepdims=True) + 1e-6)
        return wide / length, length

    img[0] = normal(raw_img)[0].astype(bf16)
    txt[0] = normal(raw_txt)[0].astype(bf16)
    pl.semaphore_wait(barrier, 30)

    sends = []

    def rows(h):
        return pl.ds(32 * h, 32)

    def go(c):
        c.start()
        sends.append(c)

    def text_part(slot, h):
        j = TSLOT[slot]
        return txt.at[j, rows(h)], txt_s.at[2 * j + h], txt_r.at[2 * j + h]

    def send_text(source, h, dy, dx):
        landing = ((source[0] - dy) % 4, (source[1] - dx) % 4)
        dst, s, r = text_part(landing, h)
        go(copy(text_part(source, h)[0], dst, s, r, at_plane(dy, dx)))

    def image_part(d, h):
        return img.at[ISLOT[0, d], rows(h)], img_s.at[2 * d + h], img_r.at[2 * d + h]

    def send_image(source, h, d):
        dst, s, r = image_part((source - d) % 8, h)
        go(copy(image_part(source, h)[0], dst, s, r, at_line(0, d)))

    arrived = set()

    def need_text(slot, h):
        if slot != (0, 0) and (slot, h) not in arrived:
            arrived.add((slot, h))
            part, s, r = text_part(slot, h)
            copy(part, part, s, r, at_plane(0, 1)).wait_recv()

    def need_image(d, h):
        if d and (d, h) not in arrived:
            arrived.add((d, h))
            part, s, r = image_part(d, h)
            copy(part, part, s, r, at_line(0, 1)).wait_recv()

    pairs = {}

    def send_pair(d):
        need_image(d, 0)
        need_image(d, 1)
        pairs[d] = copy(
            img.at[ISLOT[0, d]], img.at[ISLOT[1, d]], pair_s.at[d], pair_r.at[d], at_line(1, 0)
        )
        go(pairs[d])

    def spread(source, h):
        need_text(source, h)
        for d in ROUND:
            send_text(source, h, *((d, 0) if h == 0 else (0, d)))

    def relay(source, h):
        need_image(source, h)
        if source == 6:
            if h == 0:
                send_image(6, 0, 2)
            send_image(6, h, 1)
        else:
            if h == 1:
                send_image(2, 1, 6)
            send_image(2, h, 7)

    send_image(0, 0, 2)
    send_image(0, 0, 6)
    for d in ROUND:
        send_text((0, 0), 0, 0, d)
        send_text((0, 0), 1, d, 0)
    send_image(0, 1, 2)
    send_image(0, 1, 6)
    spread((0, 0), 0)
    spread((0, 0), 1)
    for h in range(2):
        send_image(0, h, 1)
        send_image(0, h, 7)
    send_pair(0)
    for d in (3, 1):
        spread((0, d), 0)
        spread((d, 0), 1)
    relay(6, 0)
    relay(2, 0)
    spread((0, 2), 0)
    spread((2, 0), 1)
    relay(6, 1)
    relay(2, 1)
    for d in (2, 6, 1, 7):
        send_pair(d)

    power = scale * (0.5 * math.log2(math.e))
    down, up = math.exp(-15.0), math.exp(15.0)

    def strip(i, g):
        r = pl.multiple_of(i * 128, 128)
        c = pl.multiple_of(g * 256, 256)
        left = img[pl.ds(2 * i, 2)].reshape(128, 512)
        right = txt[pl.ds(4 * g, 4)].reshape(256, 512)
        dots = lax.dot_general(left, right, NT, preferred_element_type=f32)
        f = jnp.exp2(dots * power)
        half[pl.ds(r, 128), pl.ds(c, 256)] = f
        hi = f * down
        hi = hi * hi
        lo = jnp.minimum(f, 1.0) * up
        lo = lo * lo
        row_part[0, pl.ds(r, 128), :] += hi[:, :128] + hi[:, 128:]
        row_part[1, pl.ds(r, 128), :] += lo[:, :128] + lo[:, 128:]
        col_hi[:, pl.ds(c, 256)] += jnp.sum(hi.reshape(16, 8, 256), axis=0)
        col_lo[:, pl.ds(c, 256)] += jnp.sum(lo.reshape(16, 8, 256), axis=0)

    def strips(first, last, groups):
        for g in groups:
            @pl.loop(first, last)
            def _(i):
                strip(i, g)

    def need_group(g):
        for slot in PLANE[4 * g : 4 * g + 4]:
            need_text(slot, 0)
            need_text(slot, 1)

    for d in NEAR:
        pairs[d].wait_recv()
    need_group(0)
    strips(0, 5, [0])
    need_group(1)
    strips(0, 5, [1])
    for d in FAR:
        send_pair(d)
    need_group(2)
    strips(0, 5, [2])
    for d in FAR:
        pairs[d].wait_recv()
    strips(5, 8, [0, 1, 2])
    need_group(3)
    strips(0, 8, [3])

    def log_of(hi, lo):
        return jnp.where(
            hi >= math.exp(-30.0), jnp.log(hi) + 30.0, jnp.log(lo) - 30.0
        )

    row_hi = jnp.sum(row_part[0].T, axis=0, keepdims=True)
    row_lo = jnp.sum(row_part[1].T, axis=0, keepdims=True)
    row_stat[0, :, :1024] = log_of(row_hi, row_lo)
    same = img[0].astype(f32) * txt[0].astype(f32)
    positive = scale * jnp.sum(same)
    row_stat[0, :, 1024:] = jnp.full((1, 128), positive, f32)
    for d in (4, 3, 5, 2, 6, 1, 7, 0):
        for k in range(2):
            if k or d:
                b = ISLOT[k, (8 - d) % 8]
                go(copy(row_stat.at[0], row_stat.at[b], rstat_s.at[b], rstat_r.at[b], at_line(k, d)))
    col_stat[0] = log_of(
        jnp.sum(col_hi[...], axis=0, keepdims=True), jnp.sum(col_lo[...], axis=0, keepdims=True)
    )
    for dy, dx in reversed(PLANE[1:]):
        b = TSLOT[(4 - dy) % 4, (4 - dx) % 4]
        go(copy(col_stat.at[0], col_stat.at[b], cstat_s.at[b], cstat_r.at[b], at_plane(dy, dx)))
    for j in range(1, 16):
        copy(row_stat.at[j], row_stat.at[j], rstat_s.at[j], rstat_r.at[j], at_line(0, 1)).wait_recv()
    for j in range(1, 16):
        copy(col_stat.at[j], col_stat.at[j], cstat_s.at[j], cstat_r.at[j], at_plane(0, 1)).wait_recv()

    def row_order(j):
        k, d = LINE[j]
        parts = row_stat[j, :, :1024]
        pieces = [None] * 16
        for p, (k2, d2) in enumerate(LINE):
            pieces[ISLOT[(k + k2) % 2, (d + d2) % 8]] = parts[:, p * n : p * n + n]
        return jnp.concatenate(pieces, axis=1)

    def col_order(j):
        dy, dx = PLANE[j]
        parts = col_stat[j]
        pieces = [None] * 16
        for p, (y2, x2) in enumerate(PLANE):
            pieces[TSLOT[(dy + y2) % 4, (dx + x2) % 4]] = parts[:, p * n : p * n + n]
        return jnp.concatenate(pieces, axis=1)

    def merged(parts):
        summit = functools.reduce(jnp.maximum, parts)
        total = sum(jnp.exp(p - summit) for p in parts)
        return summit + jnp.log(total)

    row_lse = merged([row_order(j) for j in range(16)])
    col_lse = merged([col_order(j) for j in range(16)])

    root = math.sqrt(0.5)
    row_factor = jnp.exp(row_lse * -0.5) * root
    col_factor = jnp.exp(col_lse * -0.5) * root
    row_scale[...] = jnp.broadcast_to(row_factor, (128, 1024)).T

    def weigh(i, carry):
        r = pl.multiple_of(i * 64, 64)
        a = row_scale[pl.ds(r, 64), :]
        for q in range(8):
            f = half[pl.ds(r, 64), q * 128 : q * 128 + 128]
            by_row = f * a
            by_col = f * col_factor[:, q * 128 : q * 128 + 128]
            weights[pl.ds(r, 64), q * 128 : q * 128 + 128] = (
                by_row * by_row + by_col * by_col
            ).astype(bf16)
        return carry

    lax.fori_loop(0, 16, weigh, 0)

    texts = txt[...].reshape(1024, 512)
    images = img[...].reshape(1024, 512)

    def image_share(first, last):
        return jnp.dot(
            weights[first * n : last * n, :], texts, preferred_element_type=f32
        ).reshape(last - first, n, 512)

    def send_share(h, first, last, to):
        img_out[first:last] = image_share(first, last).astype(bf16)
        count = last - first
        c = copy(
            img_out.at[pl.ds(first, count)], img_pair.at[pl.ds(to, count)],
            pg_s.at[h], pg_r.at[h], at_line(1, 0),
        )
        go(c)
        return c

    def text_shares(g):
        part = lax.dot_general(
            weights[:, g * 256 : g * 256 + 256], images, TN, preferred_element_type=f32
        ).reshape(4, n, 512)
        txt_out[4 * g : 4 * g + 4] = part.astype(bf16)
        for slot in PLANE[4 * g : 4 * g + 4]:
            dy, dx = slot
            j = TSLOT[slot]
            if dy:
                b = TSLOT[(4 - dy) % 4, dx]
                go(copy(
                    txt_out.at[j, rows(0)], txt_mid.at[b, rows(0)],
                    tm_s.at[2 * b], tm_r.at[2 * b], at_plane(dy, 0),
                ))
            if dx:
                b = TSLOT[dy, (4 - dx) % 4]
                go(copy(
                    txt_out.at[j, rows(1)], txt_mid.at[b, rows(1)],
                    tm_s.at[2 * b + 1], tm_r.at[2 * b + 1], at_plane(0, dx),
                ))

    far = send_share(0, 13, 16, 5)
    text_shares(3)
    near = send_share(1, 5, 10, 0)
    part = image_share(10, 13)
    far.wait_recv()
    img_out[10:13] = (part + img_pair[5:8].astype(f32)).astype(bf16)
    mids = []

    def send_mid(j, slot, h, to):
        c = copy(
            img_out.at[slot, rows(h)], img_mid.at[j, rows(h)],
            im_s.at[2 * j + h], im_r.at[2 * j + h], at_line(0, to),
        )
        go(c)
        mids.append(c)

    for h in range(2):
        send_mid(0, 10, h, 1)
        send_mid(1, 11, h, 7)
        send_mid(2, 12, h, (2, 6)[h])
    text_shares(2)
    part = image_share(0, 5)
    near.wait_recv()
    part = part + img_pair[0:5].astype(f32)
    img_own[...] = part[0]
    img_hold[...] = part[1:3]
    img_out[3:5] = part[3:5].astype(bf16)
    last = []
    for j, d in ((0, 1), (1, 7)):
        c = copy(img_out.at[3 + j], img_in.at[j], ig_s.at[j], ig_r.at[j], at_line(0, d))
        go(c)
        last.append(c)
    text_shares(1)
    text_shares(0)

    all_positive = sum(row_stat[j, :, 1024:] for j in range(16))
    row_loss[0] = jnp.full((1, 128), jnp.sum(row_lse), f32) - 2.0 * all_positive
    col_loss[0] = jnp.full((1, 128), jnp.sum(col_lse), f32)
    for dy, dx in PLANE[1:]:
        b = TSLOT[(4 - dy) % 4, (4 - dx) % 4]
        go(copy(row_loss.at[0], row_loss.at[b], rloss_s.at[b], rloss_r.at[b], at_plane(dy, dx)))
    for k, d in LINE[1:]:
        b = ISLOT[k, (8 - d) % 8]
        go(copy(col_loss.at[0], col_loss.at[b], closs_s.at[b], closs_r.at[b], at_line(k, d)))

    for c in mids:
        c.wait_recv()

    def mid(j, h):
        return img_mid[j, 32 * h : 32 * h + 32, :].astype(f32)

    for h in range(2):
        for j, d in ((0, 2), (1, 6)):
            total = img_hold[j, 32 * h : 32 * h + 32, :] + mid(j, h)
            if h == j:
                total = total + mid(2, h)
            img_send[j, 32 * h : 32 * h + 32, :] = total.astype(bf16)
            m = 2 + 2 * j + h
            c = copy(
                img_send.at[j, rows(h)], img_in.at[2 + j, rows(h)], ig_s.at[m], ig_r.at[m], at_line(0, d)
            )
            go(c)
            last.append(c)

    def need_mid(slot, h):
        m = 2 * TSLOT[slot] + h
        part = txt_mid.at[TSLOT[slot], rows(h)]
        copy(part, part, tm_s.at[m], tm_r.at[m], at_plane(0, 1)).wait_recv()

    def text_sum(d, h):
        slots = [(e, d) if h == 0 else (d, e) for e in range(4)]
        total = txt_out[TSLOT[slots[0]], 32 * h : 32 * h + 32, :].astype(f32)
        for slot in slots[1:]:
            need_mid(slot, h)
            total = total + txt_mid[TSLOT[slot], 32 * h : 32 * h + 32, :].astype(f32)
        return total

    ends = []
    for d in ROUND:
        for h in range(2):
            txt_send[d, 32 * h : 32 * h + 32, :] = text_sum(d, h).astype(bf16)
            m = 2 * (4 - d) + h
            c = copy(
                txt_send.at[d, rows(h)], txt_in.at[4 - d, rows(h)],
                tg_s.at[m], tg_r.at[m], at_plane(*((0, d) if h == 0 else (d, 0))),
            )
            go(c)
            ends.append(c)
    txt_total = jnp.concatenate([text_sum(0, 0), text_sum(0, 1)], axis=0)

    def finish(total, other, raw):
        unit, length = normal(raw)
        gradient = scale * total - scale * other.astype(f32)
        return (gradient - unit * jnp.sum(unit * gradient, axis=1, keepdims=True)) / length

    for j in range(1, 16):
        copy(row_loss.at[j], row_loss.at[j], rloss_s.at[j], rloss_r.at[j], at_line(0, 1)).wait_recv()
        copy(col_loss.at[j], col_loss.at[j], closs_s.at[j], closs_r.at[j], at_line(0, 1)).wait_recv()
    total = sum(row_loss[j] + col_loss[j] for j in range(16))
    loss_ref[...] = total / (2.0 * batch)
    for c in last:
        c.wait_recv()
    img_total = img_own[...]
    for j in range(4):
        img_total = img_total + img_in[j].astype(f32)
    img_grad_ref[...] = finish(img_total, txt[0], raw_img)
    for c in ends:
        c.wait_recv()
    for d in range(1, 4):
        txt_total = txt_total + txt_in[d].astype(f32)
    txt_grad_ref[...] = finish(txt_total, img[0], raw_txt)
    for c in sends:
        c.wait_send()


def write_out(loss_in, img_in, txt_in, loss_out, img_out, txt_out, sems):
    moves = [
        pltpu.make_async_copy(img_in, img_out, sems.at[0]),
        pltpu.make_async_copy(txt_in, txt_out, sems.at[1]),
    ]
    for c in moves:
        c.start()
    loss_out[...] = loss_in[0, :1]
    for c in moves:
        c.wait()


def on_device(image, text, logit_scale):
    batch = image.shape[0] * 256
    f32, bf16 = jnp.float32, jnp.bfloat16
    dma = pltpu.SemaphoreType.DMA
    vmem = pltpu.VMEM
    hbm = pl.BlockSpec(memory_space=pltpu.HBM)
    local = pl.BlockSpec(memory_space=vmem)
    loss, img_grad, txt_grad = pl.pallas_call(
        functools.partial(kernel, batch),
        out_shape=(
            jax.ShapeDtypeStruct((1, 128), f32),
            jax.ShapeDtypeStruct((64, 512), f32),
            jax.ShapeDtypeStruct((64, 512), f32),
        ),
        in_specs=[hbm, hbm, hbm],
        out_specs=[local] * 3,
        scratch_shapes=[
            vmem((64, 512), bf16),
            vmem((64, 512), bf16),
            pltpu.SMEM((1,), f32),
            vmem((16, 64, 512), bf16),
            vmem((16, 64, 512), bf16),
            vmem((1024, 1024), f32),
            vmem((1024, 1024), bf16),
            vmem((2, 1024, 128), f32),
            vmem((1024, 128), f32),
            vmem((8, 1024), f32),
            vmem((8, 1024), f32),
            vmem((16, 1, 1152), f32),
            vmem((16, 1, 1024), f32),
            vmem((16, 1, 128), f32),
            vmem((16, 1, 128), f32),
            vmem((16, 64, 512), bf16),
            vmem((8, 64, 512), bf16),
            vmem((2, 64, 512), f32),
            vmem((3, 64, 512), bf16),
            vmem((2, 64, 512), bf16),
            vmem((4, 64, 512), bf16),
            vmem((64, 512), f32),
            vmem((16, 64, 512), bf16),
            vmem((16, 64, 512), bf16),
            vmem((4, 64, 512), bf16),
            vmem((4, 64, 512), bf16),
            dma((3,)), dma((32,)), dma((32,)), dma((16,)), dma((16,)), dma((8,)), dma((8,)),
            dma((16,)), dma((16,)), dma((16,)), dma((16,)), dma((16,)), dma((16,)), dma((16,)), dma((16,)),
            dma((2,)), dma((2,)), dma((6,)), dma((6,)), dma((6,)), dma((6,)),
            dma((32,)), dma((32,)), dma((8,)), dma((8,)),
        ],
        compiler_params=pltpu.CompilerParams(
            collective_id=0, has_side_effects=True, vmem_limit_bytes=56 * 2**20
        ),
        cost_estimate=pl.CostEstimate(
            flops=6 * 1024 * 1024 * 512, bytes_accessed=400000, transcendentals=1024 * 1024
        ),
        name="contrast",
    )(image, text, logit_scale)
    return pl.pallas_call(
        write_out,
        out_shape=(
            jax.ShapeDtypeStruct((1,), f32),
            jax.ShapeDtypeStruct((64, 512), f32),
            jax.ShapeDtypeStruct((64, 512), f32),
        ),
        in_specs=[local, hbm, hbm],
        out_specs=[local, hbm, hbm],
        scratch_shapes=[dma((2,))],
        name="write_out",
    )(loss, img_grad, txt_grad)


def solution(mesh):
    torus = Mesh(mesh.devices.reshape(8, 4, 4, 2), AXES)
    return jax.shard_map(
        on_device,
        mesh=torus,
        in_specs=(P(AXES, None), P(AXES, None), P()),
        out_specs=(P(), P(AXES, None), P(AXES, None)),
        check_vma=False,
    )
```

```python
import functools
import math

import jax
import jax.numpy as jnp
from jax import lax
from jax.experimental import pallas as pl
from jax.experimental.pallas import tpu as pltpu
from jax.sharding import Mesh
from jax.sharding import PartitionSpec as P

MESH = pl.DeviceIdType.MESH
AXES = ("z", "y", "x", "core")
SIZE = {"z": 8, "y": 4, "x": 4, "core": 2}
NT = (((1,), (1,)), ((), ()))
TN = (((0,), (0,)), ((), ()))
NN = (((1,), (0,)), ((), ()))

NEAR = [0, 2, 6, 1, 7]
FAR = [3, 5, 4]
LINE = [(0, d) for d in NEAR] + [(1, d) for d in NEAR] + [(0, d) for d in FAR] + [(1, d) for d in FAR]
PLANE = [
    (0, 0), (0, 1), (0, 3), (1, 0), (3, 0), (0, 2), (2, 0), (1, 1),
    (1, 3), (3, 1), (3, 3), (1, 2), (3, 2), (2, 1), (2, 3), (2, 2),
]
ISLOT = {p: j for j, p in enumerate(LINE)}
TSLOT = {p: j for j, p in enumerate(PLANE)}
ROUND = (2, 1, 3)


def at_line(k, d):
    return {
        "z": lax.rem(lax.axis_index("z") + d, 8),
        "core": lax.rem(lax.axis_index("core") + k, 2),
    }


def at_plane(dy, dx):
    return {
        "y": lax.rem(lax.axis_index("y") + dy, 4),
        "x": lax.rem(lax.axis_index("x") + dx, 4),
    }


def kernel(
    batch, image_ref, text_ref, scale_ref, loss_ref, img_grad_ref, txt_grad_ref,
    raw_img, raw_txt, raw_scale, img, txt, half, weights, row_part, row_scale, col_hi, col_lo,
    row_stat, col_stat, row_loss, col_loss,
    img_out, img_pair, img_hold, img_mid, img_send, img_in, img_own,
    txt_out, txt_mid, txt_send, txt_in,
    load, txt_s, txt_r, img_s, img_r, pair_s, pair_r,
    rstat_s, rstat_r, cstat_s, cstat_r, rloss_s, rloss_r, closs_s, closs_r,
    pg_s, pg_r, im_s, im_r, ig_s, ig_r, tm_s, tm_r, tg_s, tg_r,
):
    n = 64
    f32, bf16 = jnp.float32, jnp.bfloat16

    def copy(src, dst, s, r, to):
        return pltpu.make_async_remote_copy(
            src_ref=src, dst_ref=dst, send_sem=s, recv_sem=r, device_id=to, device_id_type=MESH
        )

    barrier = pltpu.get_barrier_semaphore()
    for k, d in LINE[1:]:
        pl.semaphore_signal(barrier, inc=1, device_id=at_line(k, d), device_id_type=MESH)
    for dy, dx in PLANE[1:]:
        pl.semaphore_signal(barrier, inc=1, device_id=at_plane(dy, dx), device_id_type=MESH)
    loads = [
        pltpu.make_async_copy(image_ref, raw_img, load.at[0]),
        pltpu.make_async_copy(text_ref, raw_txt, load.at[1]),
        pltpu.make_async_copy(scale_ref, raw_scale, load.at[2]),
    ]
    for c in loads:
        c.start()
    col_hi[...] = jnp.zeros_like(col_hi)
    col_lo[...] = jnp.zeros_like(col_lo)
    row_part[...] = jnp.zeros_like(row_part)
    for c in loads:
        c.wait()
    scale = raw_scale[0]

    def normal(ref):
        wide = ref[...].astype(f32)
        length = jnp.sqrt(jnp.sum(wide * wide, axis=1, keepdims=True) + 1e-6)
        return wide / length, length

    img[0] = normal(raw_img)[0].astype(bf16)
    txt[0] = normal(raw_txt)[0].astype(bf16)
    pl.semaphore_wait(barrier, 30)

    sends = []

    def rows(h):
        return pl.ds(32 * h, 32)

    def go(c):
        c.start()
        sends.append(c)

    def text_part(slot, h):
        j = TSLOT[slot]
        return txt.at[j, rows(h)], txt_s.at[2 * j + h], txt_r.at[2 * j + h]

    def send_text(source, h, dy, dx):
        landing = ((source[0] - dy) % 4, (source[1] - dx) % 4)
        dst, s, r = text_part(landing, h)
        go(copy(text_part(source, h)[0], dst, s, r, at_plane(dy, dx)))

    def image_part(d, h):
        return img.at[ISLOT[0, d], rows(h)], img_s.at[2 * d + h], img_r.at[2 * d + h]

    def send_image(source, h, d):
        dst, s, r = image_part((source - d) % 8, h)
        go(copy(image_part(source, h)[0], dst, s, r, at_line(0, d)))

    arrived = set()

    def need_text(slot, h):
        if slot != (0, 0) and (slot, h) not in arrived:
            arrived.add((slot, h))
            part, s, r = text_part(slot, h)
            copy(part, part, s, r, at_plane(0, 1)).wait_recv()

    def need_image(d, h):
        if d and (d, h) not in arrived:
            arrived.add((d, h))
            part, s, r = image_part(d, h)
            copy(part, part, s, r, at_line(0, 1)).wait_recv()

    pairs = {}

    def send_pair(d):
        need_image(d, 0)
        need_image(d, 1)
        pairs[d] = copy(
            img.at[ISLOT[0, d]], img.at[ISLOT[1, d]], pair_s.at[d], pair_r.at[d], at_line(1, 0)
        )
        go(pairs[d])

    def spread(source, h):
        need_text(source, h)
        for d in ROUND:
            send_text(source, h, *((d, 0) if h == 0 else (0, d)))

    def relay(source, h):
        need_image(source, h)
        if source == 6:
            if h == 0:
                send_image(6, 0, 2)
            send_image(6, h, 1)
        else:
            if h == 1:
                send_image(2, 1, 6)
            send_image(2, h, 7)

    send_image(0, 0, 2)
    send_image(0, 0, 6)
    for d in ROUND:
        send_text((0, 0), 0, 0, d)
        send_text((0, 0), 1, d, 0)
    send_image(0, 1, 2)
    send_image(0, 1, 6)
    spread((0, 0), 0)
    spread((0, 0), 1)
    for h in range(2):
        send_image(0, h, 1)
        send_image(0, h, 7)
    send_pair(0)
    for d in (3, 1):
        spread((0, d), 0)
        spread((d, 0), 1)
    relay(6, 0)
    relay(2, 0)
    spread((0, 2), 0)
    spread((2, 0), 1)
    relay(6, 1)
    relay(2, 1)
    for d in (2, 6, 1, 7):
        send_pair(d)

    power = scale * (0.5 * math.log2(math.e))
    down, up = math.exp(-15.0), math.exp(15.0)

    def strips(first, last, g):
        c = pl.multiple_of(g * 256, 256)
        right = txt[pl.ds(4 * g, 4)].reshape(256, 512)
        hi_col = col_hi[:, pl.ds(c, 256)]
        lo_col = col_lo[:, pl.ds(c, 256)]
        for i in range(first, last):
            r = 128 * i
            left = img[2 * i : 2 * i + 2].reshape(128, 512)
            dots = lax.dot_general(left, right, NT, preferred_element_type=f32)
            f = jnp.exp2(dots * power)
            half[r : r + 128, pl.ds(c, 256)] = f
            hi = f * down
            hi = hi * hi
            lo = jnp.minimum(f, 1.0) * up
            lo = lo * lo
            row_part[0, r : r + 128, :] += hi[:, :128] + hi[:, 128:]
            row_part[1, r : r + 128, :] += lo[:, :128] + lo[:, 128:]
            hi_col = hi_col + jnp.sum(hi.reshape(16, 8, 256), axis=0)
            lo_col = lo_col + jnp.sum(lo.reshape(16, 8, 256), axis=0)
        col_hi[:, pl.ds(c, 256)] = hi_col
        col_lo[:, pl.ds(c, 256)] = lo_col

    def need_group(g):
        for slot in PLANE[4 * g : 4 * g + 4]:
            need_text(slot, 0)
            need_text(slot, 1)

    for d in NEAR:
        pairs[d].wait_recv()
    need_group(0)
    strips(0, 5, 0)
    need_group(1)
    strips(0, 5, 1)
    for d in FAR:
        send_pair(d)
    need_group(2)
    strips(0, 5, 2)
    for d in FAR:
        pairs[d].wait_recv()

    @pl.loop(0, 3)
    def _(g):
        strips(5, 8, g)

    need_group(3)
    strips(0, 8, 3)

    def log_of(hi, lo):
        return jnp.where(
            hi >= math.exp(-30.0), jnp.log(hi) + 30.0, jnp.log(lo) - 30.0
        )

    row_hi = jnp.sum(row_part[0].T, axis=0, keepdims=True)
    row_lo = jnp.sum(row_part[1].T, axis=0, keepdims=True)
    row_stat[0, :, :1024] = log_of(row_hi, row_lo)
    same = img[0].astype(f32) * txt[0].astype(f32)
    positive = scale * jnp.sum(same)
    row_stat[0, :, 1024:] = jnp.full((1, 128), positive, f32)
    for d in (4, 3, 5, 2, 6, 1, 7, 0):
        for k in range(2):
            if k or d:
                b = ISLOT[k, (8 - d) % 8]
                go(copy(row_stat.at[0], row_stat.at[b], rstat_s.at[b], rstat_r.at[b], at_line(k, d)))
    col_stat[0] = log_of(
        jnp.sum(col_hi[...], axis=0, keepdims=True), jnp.sum(col_lo[...], axis=0, keepdims=True)
    )
    for dy, dx in reversed(PLANE[1:]):
        b = TSLOT[(4 - dy) % 4, (4 - dx) % 4]
        go(copy(col_stat.at[0], col_stat.at[b], cstat_s.at[b], cstat_r.at[b], at_plane(dy, dx)))
    for j in range(1, 16):
        copy(row_stat.at[j], row_stat.at[j], rstat_s.at[j], rstat_r.at[j], at_line(0, 1)).wait_recv()
    for j in range(1, 16):
        copy(col_stat.at[j], col_stat.at[j], cstat_s.at[j], cstat_r.at[j], at_plane(0, 1)).wait_recv()

    def row_order(j):
        k, d = LINE[j]
        parts = row_stat[j, :, :1024]
        pieces = [None] * 16
        for p, (k2, d2) in enumerate(LINE):
            pieces[ISLOT[(k + k2) % 2, (d + d2) % 8]] = parts[:, p * n : p * n + n]
        return jnp.concatenate(pieces, axis=1)

    def col_order(j):
        dy, dx = PLANE[j]
        parts = col_stat[j]
        pieces = [None] * 16
        for p, (y2, x2) in enumerate(PLANE):
            pieces[TSLOT[(dy + y2) % 4, (dx + x2) % 4]] = parts[:, p * n : p * n + n]
        return jnp.concatenate(pieces, axis=1)

    def merged(parts):
        summit = functools.reduce(jnp.maximum, parts)
        total = sum(jnp.exp(p - summit) for p in parts)
        return summit + jnp.log(total)

    row_lse = merged([row_order(j) for j in range(16)])
    col_lse = merged([col_order(j) for j in range(16)])

    root = math.sqrt(0.5)
    row_factor = jnp.exp(row_lse * -0.5) * root
    col_factor = jnp.exp(col_lse * -0.5) * root
    row_scale[...] = jnp.broadcast_to(row_factor, (128, 1024)).T

    def weigh(i, carry):
        r = pl.multiple_of(i * 64, 64)
        a = row_scale[pl.ds(r, 64), :]
        for q in range(8):
            f = half[pl.ds(r, 64), q * 128 : q * 128 + 128]
            by_row = f * a
            by_col = f * col_factor[:, q * 128 : q * 128 + 128]
            weights[pl.ds(r, 64), q * 128 : q * 128 + 128] = (
                by_row * by_row + by_col * by_col
            ).astype(bf16)
        return carry

    lax.fori_loop(0, 16, weigh, 0)

    texts = txt[...].reshape(1024, 512)
    images = img[...].reshape(1024, 512)

    def image_share(first, last):
        return jnp.dot(
            weights[first * n : last * n, :], texts, preferred_element_type=f32
        ).reshape(last - first, n, 512)

    def send_share(h, first, last, to):
        img_out[first:last] = image_share(first, last).astype(bf16)
        count = last - first
        c = copy(
            img_out.at[pl.ds(first, count)], img_pair.at[pl.ds(to, count)],
            pg_s.at[h], pg_r.at[h], at_line(1, 0),
        )
        go(c)
        return c

    def text_shares(g):
        part = lax.dot_general(
            weights[:, g * 256 : g * 256 + 256], images, TN, preferred_element_type=f32
        ).reshape(4, n, 512)
        txt_out[4 * g : 4 * g + 4] = part.astype(bf16)
        for slot in PLANE[4 * g : 4 * g + 4]:
            dy, dx = slot
            j = TSLOT[slot]
            if dy:
                b = TSLOT[(4 - dy) % 4, dx]
                go(copy(
                    txt_out.at[j, rows(0)], txt_mid.at[b, rows(0)],
                    tm_s.at[2 * b], tm_r.at[2 * b], at_plane(dy, 0),
                ))
            if dx:
                b = TSLOT[dy, (4 - dx) % 4]
                go(copy(
                    txt_out.at[j, rows(1)], txt_mid.at[b, rows(1)],
                    tm_s.at[2 * b + 1], tm_r.at[2 * b + 1], at_plane(0, dx),
                ))

    far = send_share(0, 13, 16, 5)
    text_shares(3)
    near = send_share(1, 5, 10, 0)
    part = image_share(10, 13)
    far.wait_recv()
    img_out[10:13] = (part + img_pair[5:8].astype(f32)).astype(bf16)
    mids = []

    def send_mid(j, slot, h, to):
        c = copy(
            img_out.at[slot, rows(h)], img_mid.at[j, rows(h)],
            im_s.at[2 * j + h], im_r.at[2 * j + h], at_line(0, to),
        )
        go(c)
        mids.append(c)

    for h in range(2):
        send_mid(0, 10, h, 1)
        send_mid(1, 11, h, 7)
        send_mid(2, 12, h, (2, 6)[h])
    text_shares(2)
    part = image_share(0, 5)
    near.wait_recv()
    part = part + img_pair[0:5].astype(f32)
    img_own[...] = part[0]
    img_hold[...] = part[1:3]
    img_out[3:5] = part[3:5].astype(bf16)
    last = []
    for j, d in ((0, 1), (1, 7)):
        c = copy(img_out.at[3 + j], img_in.at[j], ig_s.at[j], ig_r.at[j], at_line(0, d))
        go(c)
        last.append(c)
    text_shares(1)
    text_shares(0)

    all_positive = sum(row_stat[j, :, 1024:] for j in range(16))
    row_loss[0] = jnp.full((1, 128), jnp.sum(row_lse), f32) - 2.0 * all_positive
    col_loss[0] = jnp.full((1, 128), jnp.sum(col_lse), f32)
    for dy, dx in PLANE[1:]:
        b = TSLOT[(4 - dy) % 4, (4 - dx) % 4]
        go(copy(row_loss.at[0], row_loss.at[b], rloss_s.at[b], rloss_r.at[b], at_plane(dy, dx)))
    for k, d in LINE[1:]:
        b = ISLOT[k, (8 - d) % 8]
        go(copy(col_loss.at[0], col_loss.at[b], closs_s.at[b], closs_r.at[b], at_line(k, d)))

    for c in mids:
        c.wait_recv()

    def mid(j, h):
        return img_mid[j, 32 * h : 32 * h + 32, :].astype(f32)

    for h in range(2):
        for j, d in ((0, 2), (1, 6)):
            total = img_hold[j, 32 * h : 32 * h + 32, :] + mid(j, h)
            if h == j:
                total = total + mid(2, h)
            img_send[j, 32 * h : 32 * h + 32, :] = total.astype(bf16)
            m = 2 + 2 * j + h
            c = copy(
                img_send.at[j, rows(h)], img_in.at[2 + j, rows(h)], ig_s.at[m], ig_r.at[m], at_line(0, d)
            )
            go(c)
            last.append(c)

    def need_mid(slot, h):
        m = 2 * TSLOT[slot] + h
        part = txt_mid.at[TSLOT[slot], rows(h)]
        copy(part, part, tm_s.at[m], tm_r.at[m], at_plane(0, 1)).wait_recv()

    def text_sum(d, h):
        slots = [(e, d) if h == 0 else (d, e) for e in range(4)]
        total = txt_out[TSLOT[slots[0]], 32 * h : 32 * h + 32, :].astype(f32)
        for slot in slots[1:]:
            need_mid(slot, h)
            total = total + txt_mid[TSLOT[slot], 32 * h : 32 * h + 32, :].astype(f32)
        return total

    ends = []
    for d in ROUND:
        for h in range(2):
            txt_send[d, 32 * h : 32 * h + 32, :] = text_sum(d, h).astype(bf16)
            m = 2 * (4 - d) + h
            c = copy(
                txt_send.at[d, rows(h)], txt_in.at[4 - d, rows(h)],
                tg_s.at[m], tg_r.at[m], at_plane(*((0, d) if h == 0 else (d, 0))),
            )
            go(c)
            ends.append(c)
    txt_total = jnp.concatenate([text_sum(0, 0), text_sum(0, 1)], axis=0)

    def finish(total, other, raw):
        unit, length = normal(raw)
        gradient = scale * total - scale * other.astype(f32)
        return (gradient - unit * jnp.sum(unit * gradient, axis=1, keepdims=True)) / length

    for j in range(1, 16):
        copy(row_loss.at[j], row_loss.at[j], rloss_s.at[j], rloss_r.at[j], at_line(0, 1)).wait_recv()
        copy(col_loss.at[j], col_loss.at[j], closs_s.at[j], closs_r.at[j], at_line(0, 1)).wait_recv()
    total = sum(row_loss[j] + col_loss[j] for j in range(16))
    loss_ref[...] = total / (2.0 * batch)
    for c in last:
        c.wait_recv()
    img_total = img_own[...]
    for j in range(4):
        img_total = img_total + img_in[j].astype(f32)
    img_grad_ref[...] = finish(img_total, txt[0], raw_img)
    for c in ends:
        c.wait_recv()
    for d in range(1, 4):
        txt_total = txt_total + txt_in[d].astype(f32)
    txt_grad_ref[...] = finish(txt_total, img[0], raw_txt)
    for c in sends:
        c.wait_send()


def write_out(loss_in, img_in, txt_in, loss_out, img_out, txt_out):
    loss_out[...] = loss_in[0, :1]
    img_out[...] = img_in[...]
    txt_out[...] = txt_in[...]


def on_device(image, text, logit_scale):
    batch = image.shape[0] * 256
    f32, bf16 = jnp.float32, jnp.bfloat16
    dma = pltpu.SemaphoreType.DMA
    vmem = pltpu.VMEM
    hbm = pl.BlockSpec(memory_space=pltpu.HBM)
    local = pl.BlockSpec(memory_space=vmem)
    loss, img_grad, txt_grad = pl.pallas_call(
        functools.partial(kernel, batch),
        out_shape=(
            jax.ShapeDtypeStruct((1, 128), f32),
            jax.ShapeDtypeStruct((64, 512), f32),
            jax.ShapeDtypeStruct((64, 512), f32),
        ),
        in_specs=[hbm, hbm, hbm],
        out_specs=[local] * 3,
        scratch_shapes=[
            vmem((64, 512), bf16),
            vmem((64, 512), bf16),
            pltpu.SMEM((1,), f32),
            vmem((16, 64, 512), bf16),
            vmem((16, 64, 512), bf16),
            vmem((1024, 1024), f32),
            vmem((1024, 1024), bf16),
            vmem((2, 1024, 128), f32),
            vmem((1024, 128), f32),
            vmem((8, 1024), f32),
            vmem((8, 1024), f32),
            vmem((16, 1, 1152), f32),
            vmem((16, 1, 1024), f32),
            vmem((16, 1, 128), f32),
            vmem((16, 1, 128), f32),
            vmem((16, 64, 512), bf16),
            vmem((8, 64, 512), bf16),
            vmem((2, 64, 512), f32),
            vmem((3, 64, 512), bf16),
            vmem((2, 64, 512), bf16),
            vmem((4, 64, 512), bf16),
            vmem((64, 512), f32),
            vmem((16, 64, 512), bf16),
            vmem((16, 64, 512), bf16),
            vmem((4, 64, 512), bf16),
            vmem((4, 64, 512), bf16),
            dma((3,)), dma((32,)), dma((32,)), dma((16,)), dma((16,)), dma((8,)), dma((8,)),
            dma((16,)), dma((16,)), dma((16,)), dma((16,)), dma((16,)), dma((16,)), dma((16,)), dma((16,)),
            dma((2,)), dma((2,)), dma((6,)), dma((6,)), dma((6,)), dma((6,)),
            dma((32,)), dma((32,)), dma((8,)), dma((8,)),
        ],
        compiler_params=pltpu.CompilerParams(
            collective_id=0, has_side_effects=True, vmem_limit_bytes=56 * 2**20
        ),
        cost_estimate=pl.CostEstimate(
            flops=6 * 1024 * 1024 * 512, bytes_accessed=400000, transcendentals=1024 * 1024
        ),
        name="contrast",
    )(image, text, logit_scale)
    return pl.pallas_call(
        write_out,
        out_shape=(
            jax.ShapeDtypeStruct((1,), f32),
            jax.ShapeDtypeStruct((64, 512), f32),
            jax.ShapeDtypeStruct((64, 512), f32),
        ),
        in_specs=[local] * 3,
        out_specs=[local] * 3,
        name="write_out",
    )(loss, img_grad, txt_grad)


def solution(mesh):
    torus = Mesh(mesh.devices.reshape(8, 4, 4, 2), AXES)
    return jax.shard_map(
        on_device,
        mesh=torus,
        in_specs=(P(AXES, None), P(AXES, None), P()),
        out_specs=(P(), P(AXES, None), P(AXES, None)),
        check_vma=False,
    )
```

```python
import functools
import math

import jax
import jax.numpy as jnp
from jax import lax
from jax.experimental import pallas as pl
from jax.experimental.pallas import tpu as pltpu
from jax.sharding import Mesh
from jax.sharding import PartitionSpec as P

MESH = pl.DeviceIdType.MESH
AXES = ("z", "y", "x", "core")
SIZE = {"z": 8, "y": 4, "x": 4, "core": 2}
NT = (((1,), (1,)), ((), ()))
TN = (((0,), (0,)), ((), ()))
NN = (((1,), (0,)), ((), ()))

NEAR = [0, 2, 6, 1, 7]
FAR = [3, 5, 4]
LINE = [(0, d) for d in NEAR] + [(1, d) for d in NEAR] + [(0, d) for d in FAR] + [(1, d) for d in FAR]
PLANE = [
    (0, 0), (0, 1), (0, 3), (1, 0), (3, 0), (0, 2), (2, 0), (1, 1),
    (1, 3), (3, 1), (3, 3), (1, 2), (3, 2), (2, 1), (2, 3), (2, 2),
]
ISLOT = {p: j for j, p in enumerate(LINE)}
TSLOT = {p: j for j, p in enumerate(PLANE)}
ROUND = (2, 1, 3)


def at_line(k, d):
    return {
        "z": lax.rem(lax.axis_index("z") + d, 8),
        "core": lax.rem(lax.axis_index("core") + k, 2),
    }


def at_plane(dy, dx):
    return {
        "y": lax.rem(lax.axis_index("y") + dy, 4),
        "x": lax.rem(lax.axis_index("x") + dx, 4),
    }


def kernel(
    batch, image_ref, text_ref, scale_ref, loss_ref, img_grad_ref, txt_grad_ref,
    raw_img, raw_txt, raw_scale, img, txt, half, weights, row_part, row_scale, col_hi, col_lo,
    row_stat, col_stat, row_loss, col_loss,
    img_out, img_pair, img_hold, img_mid, img_send, img_in, img_own,
    txt_out, txt_mid, txt_send, txt_in,
    load, sent, txt_r, img_r, pair_r, stat_r, pg_r, im_r, ig_r, tm_r, tg_r,
):
    n = 64
    f32, bf16 = jnp.float32, jnp.bfloat16

    def copy(src, dst, s, r, to):
        return pltpu.make_async_remote_copy(
            src_ref=src, dst_ref=dst, send_sem=s, recv_sem=r, device_id=to, device_id_type=MESH
        )

    barrier = pltpu.get_barrier_semaphore()
    for k, d in LINE[1:]:
        pl.semaphore_signal(barrier, inc=1, device_id=at_line(k, d), device_id_type=MESH)
    for dy, dx in PLANE[1:]:
        pl.semaphore_signal(barrier, inc=1, device_id=at_plane(dy, dx), device_id_type=MESH)
    loads = [
        pltpu.make_async_copy(image_ref, raw_img, load.at[0]),
        pltpu.make_async_copy(text_ref, raw_txt, load.at[1]),
        pltpu.make_async_copy(scale_ref, raw_scale, load.at[2]),
    ]
    for c in loads:
        c.start()
    col_hi[...] = jnp.zeros_like(col_hi)
    col_lo[...] = jnp.zeros_like(col_lo)
    row_part[...] = jnp.zeros_like(row_part)
    for c in loads:
        c.wait()
    scale = raw_scale[0]

    def normal(ref):
        wide = ref[...].astype(f32)
        length = jnp.sqrt(jnp.sum(wide * wide, axis=1, keepdims=True) + 1e-6)
        return wide / length, length

    img[0] = normal(raw_img)[0].astype(bf16)
    txt[0] = normal(raw_txt)[0].astype(bf16)
    pl.semaphore_wait(barrier, 30)

    TXT, IMG, PAIR, RSTAT, CSTAT, RLOSS, CLOSS, SHARE, MID, LAST, TMID, END = range(12)

    def rows(h):
        return pl.ds(32 * h, 32)

    def take(ref, sem):
        copy(ref, ref, sent.at[0], sem, at_line(1, 0)).wait_recv()

    def drain(ref, kind):
        copy(ref, ref, sent.at[kind], pair_r.at[0], at_line(1, 0)).wait_send()

    first_hop = [((0, d), 0) for d in (1, 2, 3)] + [((d, 0), 1) for d in (1, 2, 3)]

    def text_sem(slot, h):
        if (slot, h) in first_hop:
            return txt_r.at[first_hop.index((slot, h))]
        return txt_r.at[6 + TSLOT[slot] // 4]

    def send_text(source, h, dy, dx):
        landing = ((source[0] - dy) % 4, (source[1] - dx) % 4)
        copy(
            txt.at[TSLOT[source], rows(h)], txt.at[TSLOT[landing], rows(h)],
            sent.at[TXT], text_sem(landing, h), at_plane(dy, dx),
        ).start()

    def image_sem(d, h):
        return img_r.at[{2: h, 6: 2 + h, 1: 4, 7: 5, 3: 6, 5: 7, 4: 8}[d]]

    def send_image(source, h, d):
        landing = (source - d) % 8
        copy(
            img.at[ISLOT[0, source], rows(h)], img.at[ISLOT[0, landing], rows(h)],
            sent.at[IMG], image_sem(landing, h), at_line(0, d),
        ).start()

    def send_pair(d):
        if d in (1, 7, 3, 5, 4):
            take(img.at[ISLOT[0, d]], image_sem(d, 0))
        copy(
            img.at[ISLOT[0, d]], img.at[ISLOT[1, d]],
            sent.at[PAIR], pair_r.at[int(d in FAR)], at_line(1, 0),
        ).start()

    def spread(source, h):
        if (source, h) in first_hop:
            take(txt.at[TSLOT[source], rows(h)], text_sem(source, h))
        for d in ROUND:
            send_text(source, h, *((d, 0) if h == 0 else (0, d)))

    def relay(source, h):
        take(img.at[ISLOT[0, source], rows(h)], image_sem(source, h))
        if source == 6:
            if h == 0:
                send_image(6, 0, 2)
            send_image(6, h, 1)
        else:
            if h == 1:
                send_image(2, 1, 6)
            send_image(2, h, 7)

    send_image(0, 0, 2)
    send_image(0, 0, 6)
    send_image(0, 1, 2)
    send_image(0, 1, 6)
    for d in (1, 3, 2):
        send_text((0, 0), 0, 0, d)
        send_text((0, 0), 1, d, 0)
    for h in range(2):
        send_image(0, h, 1)
        send_image(0, h, 7)
    spread((0, 0), 0)
    spread((0, 0), 1)
    send_pair(0)
    relay(6, 0)
    relay(2, 0)
    for d in (3, 1):
        spread((0, d), 0)
        spread((d, 0), 1)
    relay(6, 1)
    relay(2, 1)
    spread((0, 2), 0)
    spread((2, 0), 1)
    for d in (2, 6, 1, 7):
        send_pair(d)

    power = scale * (0.5 * math.log2(math.e))
    down, up = math.exp(-15.0), math.exp(15.0)

    def strips(first, last, g):
        c = pl.multiple_of(g * 256, 256)
        right = txt[pl.ds(4 * g, 4)].reshape(256, 512)
        hi_col = col_hi[:, pl.ds(c, 256)]
        lo_col = col_lo[:, pl.ds(c, 256)]
        for i in range(first, last):
            r = 128 * i
            left = img[2 * i : 2 * i + 2].reshape(128, 512)
            dots = lax.dot_general(left, right, NT, preferred_element_type=f32)
            f = jnp.exp2(dots * power)
            half[r : r + 128, pl.ds(c, 256)] = f
            hi = f * down
            hi = hi * hi
            lo = jnp.minimum(f, 1.0) * up
            lo = lo * lo
            row_part[0, r : r + 128, :] += hi[:, :128] + hi[:, 128:]
            row_part[1, r : r + 128, :] += lo[:, :128] + lo[:, 128:]
            hi_col = hi_col + jnp.sum(hi.reshape(16, 8, 256), axis=0)
            lo_col = lo_col + jnp.sum(lo.reshape(16, 8, 256), axis=0)
        col_hi[:, pl.ds(c, 256)] = hi_col
        col_lo[:, pl.ds(c, 256)] = lo_col

    def need_group(g):
        count = 8 - sum(TSLOT[slot] // 4 == g for slot, _ in first_hop) - 2 * (g == 0)
        take(img.at[pl.ds(0, count), rows(0)], txt_r.at[6 + g])

    take(img.at[pl.ds(0, 5)], pair_r.at[0])
    need_group(0)
    strips(0, 5, 0)
    need_group(1)
    strips(0, 5, 1)
    need_group(2)
    strips(0, 5, 2)
    for d in FAR:
        send_pair(d)
    need_group(3)
    strips(0, 5, 3)

    @pl.loop(0, 4)
    def _(g):
        strips(5, 6, g)

    take(img.at[pl.ds(0, 3)], pair_r.at[1])

    @pl.loop(0, 4)
    def _(g):
        strips(6, 8, g)

    def log_of(hi, lo):
        return jnp.where(
            hi >= math.exp(-30.0), jnp.log(hi) + 30.0, jnp.log(lo) - 30.0
        )

    row_hi = jnp.sum(row_part[0].T, axis=0, keepdims=True)
    row_lo = jnp.sum(row_part[1].T, axis=0, keepdims=True)
    row_stat[0, :, :1024] = log_of(row_hi, row_lo)
    same = img[0].astype(f32) * txt[0].astype(f32)
    positive = scale * jnp.sum(same)
    row_stat[0, :, 1024:] = jnp.full((1, 128), positive, f32)
    for d in (4, 3, 5, 2, 6, 1, 7, 0):
        for k in range(2):
            if k or d:
                b = ISLOT[k, (8 - d) % 8]
                copy(row_stat.at[0], row_stat.at[b], sent.at[RSTAT], stat_r.at[0], at_line(k, d)).start()
    col_stat[0] = log_of(
        jnp.sum(col_hi[...], axis=0, keepdims=True), jnp.sum(col_lo[...], axis=0, keepdims=True)
    )
    for dy, dx in reversed(PLANE[1:]):
        b = TSLOT[(4 - dy) % 4, (4 - dx) % 4]
        copy(col_stat.at[0], col_stat.at[b], sent.at[CSTAT], stat_r.at[1], at_plane(dy, dx)).start()
    take(row_stat.at[pl.ds(1, 15)], stat_r.at[0])
    take(col_stat.at[pl.ds(1, 15)], stat_r.at[1])

    def row_order(j):
        k, d = LINE[j]
        parts = row_stat[j, :, :1024]
        pieces = [None] * 16
        for p, (k2, d2) in enumerate(LINE):
            pieces[ISLOT[(k + k2) % 2, (d + d2) % 8]] = parts[:, p * n : p * n + n]
        return jnp.concatenate(pieces, axis=1)

    def col_order(j):
        dy, dx = PLANE[j]
        parts = col_stat[j]
        pieces = [None] * 16
        for p, (y2, x2) in enumerate(PLANE):
            pieces[TSLOT[(dy + y2) % 4, (dx + x2) % 4]] = parts[:, p * n : p * n + n]
        return jnp.concatenate(pieces, axis=1)

    def merged(parts):
        summit = functools.reduce(jnp.maximum, parts)
        total = sum(jnp.exp(p - summit) for p in parts)
        return summit + jnp.log(total)

    row_lse = merged([row_order(j) for j in range(16)])
    col_lse = merged([col_order(j) for j in range(16)])

    root = math.sqrt(0.5)
    row_factor = jnp.exp(row_lse * -0.5) * root
    col_factor = jnp.exp(col_lse * -0.5) * root
    row_scale[...] = jnp.broadcast_to(row_factor, (128, 1024)).T

    def weigh(first, last):
        for r in range(64 * first, 64 * last, 64):
            a = row_scale[r : r + 64, :]
            for q in range(0, 1024, 128):
                f = half[r : r + 64, q : q + 128]
                by_row = f * a
                by_col = f * col_factor[:, q : q + 128]
                weights[r : r + 64, q : q + 128] = (by_row * by_row + by_col * by_col).astype(bf16)

    texts = txt[...].reshape(1024, 512)
    images = img[...].reshape(1024, 512)

    def image_share(first, last):
        return jnp.dot(
            weights[first * n : last * n, :], texts, preferred_element_type=f32
        ).reshape(last - first, n, 512)

    def send_share(h, first, last, to):
        img_out[first:last] = image_share(first, last).astype(bf16)
        count = last - first
        copy(
            img_out.at[pl.ds(first, count)], img_pair.at[pl.ds(to, count)],
            sent.at[SHARE], pg_r.at[h], at_line(1, 0),
        ).start()

    def text_shares(g):
        part = lax.dot_general(
            weights[:, g * 256 : g * 256 + 256], images, TN, preferred_element_type=f32
        ).reshape(4, n, 512)
        txt_out[4 * g : 4 * g + 4] = part.astype(bf16)
        for slot in PLANE[4 * g : 4 * g + 4]:
            dy, dx = slot
            j = TSLOT[slot]
            if dy:
                b = TSLOT[(4 - dy) % 4, dx]
                copy(
                    txt_out.at[j, rows(0)], txt_mid.at[b, rows(0)],
                    sent.at[TMID], tm_r.at[2 * dx], at_plane(dy, 0),
                ).start()
            if dx:
                b = TSLOT[dy, (4 - dx) % 4]
                copy(
                    txt_out.at[j, rows(1)], txt_mid.at[b, rows(1)],
                    sent.at[TMID], tm_r.at[2 * dy + 1], at_plane(0, dx),
                ).start()

    def send_mid(j, slot, h, to):
        copy(
            img_out.at[slot, rows(h)], img_mid.at[j, rows(h)],
            sent.at[MID], im_r.at[h], at_line(0, to),
        ).start()

    weigh(13, 16)
    send_share(0, 13, 16, 5)
    weigh(10, 13)
    part = image_share(10, 13)
    weigh(5, 10)
    take(img_pair.at[pl.ds(5, 3)], pg_r.at[0])
    img_out[10:13] = (part + img_pair[5:8].astype(f32)).astype(bf16)
    for h in range(2):
        send_mid(0, 10, h, 1)
        send_mid(1, 11, h, 7)
        send_mid(2, 12, h, (2, 6)[h])
    send_share(1, 5, 10, 0)
    weigh(0, 5)
    text_shares(3)
    part = image_share(0, 5)
    take(img_pair.at[pl.ds(0, 5)], pg_r.at[1])
    part = part + img_pair[0:5].astype(f32)
    img_own[...] = part[0]
    img_hold[...] = part[1:3]
    img_out[3:5] = part[3:5].astype(bf16)
    for j, d in ((0, 1), (1, 7)):
        copy(img_out.at[3 + j], img_in.at[j], sent.at[LAST], ig_r.at[0], at_line(0, d)).start()
    text_shares(2)
    text_shares(1)
    text_shares(0)

    all_positive = sum(row_stat[j, :, 1024:] for j in range(16))
    row_loss[0] = jnp.full((1, 128), jnp.sum(row_lse), f32) - 2.0 * all_positive
    col_loss[0] = jnp.full((1, 128), jnp.sum(col_lse), f32)
    for dy, dx in PLANE[1:]:
        b = TSLOT[(4 - dy) % 4, (4 - dx) % 4]
        copy(row_loss.at[0], row_loss.at[b], sent.at[RLOSS], stat_r.at[2], at_plane(dy, dx)).start()
    for k, d in LINE[1:]:
        b = ISLOT[k, (8 - d) % 8]
        copy(col_loss.at[0], col_loss.at[b], sent.at[CLOSS], stat_r.at[3], at_line(k, d)).start()

    def mid(j, h):
        return img_mid[j, 32 * h : 32 * h + 32, :].astype(f32)

    for h in range(2):
        take(img_mid.at[pl.ds(0, 3), rows(h)], im_r.at[h])
        for j, d in ((0, 2), (1, 6)):
            total = img_hold[j, 32 * h : 32 * h + 32, :] + mid(j, h)
            if h == j:
                total = total + mid(2, h)
            img_send[j, 32 * h : 32 * h + 32, :] = total.astype(bf16)
            copy(
                img_send.at[j, rows(h)], img_in.at[2 + j, rows(h)],
                sent.at[LAST], ig_r.at[0], at_line(0, d),
            ).start()

    def text_sum(d, h):
        slots = [(e, d) if h == 0 else (d, e) for e in range(4)]
        take(txt_mid.at[pl.ds(0, 3), rows(h)], tm_r.at[2 * d + h])
        total = txt_out[TSLOT[slots[0]], 32 * h : 32 * h + 32, :].astype(f32)
        for slot in slots[1:]:
            total = total + txt_mid[TSLOT[slot], 32 * h : 32 * h + 32, :].astype(f32)
        return total

    for d in ROUND:
        for h in range(2):
            txt_send[d, 32 * h : 32 * h + 32, :] = text_sum(d, h).astype(bf16)
            copy(
                txt_send.at[d, rows(h)], txt_in.at[4 - d, rows(h)],
                sent.at[END], tg_r.at[0], at_plane(*((0, d) if h == 0 else (d, 0))),
            ).start()
    txt_total = jnp.concatenate([text_sum(0, 0), text_sum(0, 1)], axis=0)

    def finish(total, other, raw):
        unit, length = normal(raw)
        gradient = scale * total - scale * other.astype(f32)
        return (gradient - unit * jnp.sum(unit * gradient, axis=1, keepdims=True)) / length

    take(row_loss.at[pl.ds(1, 15)], stat_r.at[2])
    take(col_loss.at[pl.ds(1, 15)], stat_r.at[3])
    total = sum(row_loss[j] + col_loss[j] for j in range(16))
    loss_ref[...] = total / (2.0 * batch)
    take(img_in, ig_r.at[0])
    img_total = img_own[...]
    for j in range(4):
        img_total = img_total + img_in[j].astype(f32)
    img_grad_ref[...] = finish(img_total, txt[0], raw_img)
    take(txt_in.at[pl.ds(1, 3)], tg_r.at[0])
    for d in range(1, 4):
        txt_total = txt_total + txt_in[d].astype(f32)
    txt_grad_ref[...] = finish(txt_total, img[0], raw_txt)
    drain(txt.at[pl.ds(0, 15)], TXT)
    drain(img.at[pl.ds(0, 7)], IMG)
    drain(img.at[pl.ds(0, 8)], PAIR)
    drain(row_stat.at[pl.ds(1, 15)], RSTAT)
    drain(col_stat.at[pl.ds(1, 15)], CSTAT)
    drain(row_loss.at[pl.ds(1, 15)], RLOSS)
    drain(col_loss.at[pl.ds(1, 15)], CLOSS)
    drain(img_pair, SHARE)
    drain(img_mid, MID)
    drain(img_in, LAST)
    drain(txt.at[pl.ds(0, 12)], TMID)
    drain(txt_in.at[pl.ds(1, 3)], END)


def write_out(loss_in, img_in, txt_in, loss_out, img_out, txt_out):
    loss_out[...] = loss_in[0, :1]
    img_out[...] = img_in[...]
    txt_out[...] = txt_in[...]


def on_device(image, text, logit_scale):
    batch = image.shape[0] * 256
    f32, bf16 = jnp.float32, jnp.bfloat16
    dma = pltpu.SemaphoreType.DMA
    vmem = pltpu.VMEM
    hbm = pl.BlockSpec(memory_space=pltpu.HBM)
    local = pl.BlockSpec(memory_space=vmem)
    loss, img_grad, txt_grad = pl.pallas_call(
        functools.partial(kernel, batch),
        out_shape=(
            jax.ShapeDtypeStruct((1, 128), f32),
            jax.ShapeDtypeStruct((64, 512), f32),
            jax.ShapeDtypeStruct((64, 512), f32),
        ),
        in_specs=[hbm, hbm, hbm],
        out_specs=[local] * 3,
        scratch_shapes=[
            vmem((64, 512), bf16),
            vmem((64, 512), bf16),
            pltpu.SMEM((1,), f32),
            vmem((16, 64, 512), bf16),
            vmem((16, 64, 512), bf16),
            vmem((1024, 1024), f32),
            vmem((1024, 1024), bf16),
            vmem((2, 1024, 128), f32),
            vmem((1024, 128), f32),
            vmem((8, 1024), f32),
            vmem((8, 1024), f32),
            vmem((16, 1, 1152), f32),
            vmem((16, 1, 1024), f32),
            vmem((16, 1, 128), f32),
            vmem((16, 1, 128), f32),
            vmem((16, 64, 512), bf16),
            vmem((8, 64, 512), bf16),
            vmem((2, 64, 512), f32),
            vmem((3, 64, 512), bf16),
            vmem((2, 64, 512), bf16),
            vmem((4, 64, 512), bf16),
            vmem((64, 512), f32),
            vmem((16, 64, 512), bf16),
            vmem((16, 64, 512), bf16),
            vmem((4, 64, 512), bf16),
            vmem((4, 64, 512), bf16),
            dma((3,)), dma((12,)), dma((10,)), dma((9,)), dma((2,)), dma((4,)), dma((2,)), dma((2,)),
            dma((1,)), dma((8,)), dma((1,)),
        ],
        compiler_params=pltpu.CompilerParams(
            collective_id=0, has_side_effects=True, vmem_limit_bytes=56 * 2**20
        ),
        cost_estimate=pl.CostEstimate(
            flops=6 * 1024 * 1024 * 512, bytes_accessed=400000, transcendentals=1024 * 1024
        ),
        name="contrast",
    )(image, text, logit_scale)
    return pl.pallas_call(
        write_out,
        out_shape=(
            jax.ShapeDtypeStruct((1,), f32),
            jax.ShapeDtypeStruct((64, 512), f32),
            jax.ShapeDtypeStruct((64, 512), f32),
        ),
        in_specs=[local] * 3,
        out_specs=[local] * 3,
        name="write_out",
    )(loss, img_grad, txt_grad)


def solution(mesh):
    torus = Mesh(mesh.devices.reshape(8, 4, 4, 2), AXES)
    return jax.shard_map(
        on_device,
        mesh=torus,
        in_specs=(P(AXES, None), P(AXES, None), P()),
        out_specs=(P(), P(AXES, None), P(AXES, None)),
        check_vma=False,
    )
```

```python
import functools
import math

import jax
import jax.numpy as jnp
from jax import lax
from jax.experimental import pallas as pl
from jax.experimental.pallas import tpu as pltpu
from jax.sharding import Mesh
from jax.sharding import PartitionSpec as P

MESH = pl.DeviceIdType.MESH
AXES = ("z", "y", "x", "core")
SIZE = {"z": 8, "y": 4, "x": 4, "core": 2}
NT = (((1,), (1,)), ((), ()))
TN = (((0,), (0,)), ((), ()))
NN = (((1,), (0,)), ((), ()))

NEAR = [0, 2, 6, 1, 7]
FAR = [3, 5, 4]
LINE = [(0, d) for d in NEAR] + [(1, d) for d in NEAR] + [(0, d) for d in FAR] + [(1, d) for d in FAR]
PLANE = [
    (0, 0), (0, 1), (0, 3), (1, 0), (3, 0), (0, 2), (2, 0), (1, 1),
    (1, 3), (3, 1), (3, 3), (1, 2), (3, 2), (2, 1), (2, 3), (2, 2),
]
ISLOT = {p: j for j, p in enumerate(LINE)}
TSLOT = {p: j for j, p in enumerate(PLANE)}
ROUND = (2, 1, 3)


def at_line(k, d):
    return {
        "z": lax.rem(lax.axis_index("z") + d, 8),
        "core": lax.rem(lax.axis_index("core") + k, 2),
    }


def at_plane(dy, dx):
    return {
        "y": lax.rem(lax.axis_index("y") + dy, 4),
        "x": lax.rem(lax.axis_index("x") + dx, 4),
    }


def kernel(
    batch, image_ref, text_ref, scale_ref, loss_ref, img_grad_ref, txt_grad_ref,
    raw_img, raw_txt, raw_scale, unit, over_length, img, txt, half, weights, row_part, row_scale, col_hi, col_lo,
    row_stat, col_stat, row_loss, col_loss,
    img_out, img_pair, img_hold, img_mid, img_send, img_in, img_own,
    txt_out, txt_mid, txt_send, txt_in,
    load, sent, txt_r, img_r, pair_r, stat_r, pg_r, im_r, ig_r, tm_r, tg_r,
):
    n = 64
    f32, bf16 = jnp.float32, jnp.bfloat16

    def copy(src, dst, s, r, to):
        return pltpu.make_async_remote_copy(
            src_ref=src, dst_ref=dst, send_sem=s, recv_sem=r, device_id=to, device_id_type=MESH
        )

    barrier = pltpu.get_barrier_semaphore()
    for k, d in LINE[1:]:
        pl.semaphore_signal(barrier, inc=1, device_id=at_line(k, d), device_id_type=MESH)
    for dy, dx in PLANE[1:]:
        pl.semaphore_signal(barrier, inc=1, device_id=at_plane(dy, dx), device_id_type=MESH)
    loads = [
        pltpu.make_async_copy(image_ref, raw_img, load.at[0]),
        pltpu.make_async_copy(text_ref, raw_txt, load.at[1]),
        pltpu.make_async_copy(scale_ref, raw_scale, load.at[2]),
    ]
    for c in loads:
        c.start()
    col_hi[...] = jnp.zeros_like(col_hi)
    col_lo[...] = jnp.zeros_like(col_lo)
    row_part[...] = jnp.zeros_like(row_part)
    for c in loads:
        c.wait()
    scale = raw_scale[0]

    def normal(ref):
        wide = ref[...].astype(f32)
        length = jnp.sqrt(jnp.sum(wide * wide, axis=1, keepdims=True) + 1e-6)
        return wide / length, length

    img[0] = normal(raw_img)[0].astype(bf16)
    txt[0] = normal(raw_txt)[0].astype(bf16)
    pl.semaphore_wait(barrier, 30)

    TXT, IMG, PAIR, RSTAT, CSTAT, RLOSS, CLOSS, SHARE, MID, LAST, TMID, END = range(12)

    def rows(h):
        return pl.ds(32 * h, 32)

    def take(ref, sem):
        copy(ref, ref, sent.at[0], sem, at_line(1, 0)).wait_recv()

    def drain(ref, kind):
        copy(ref, ref, sent.at[kind], pair_r.at[0], at_line(1, 0)).wait_send()

    first_hop = [((0, d), 0) for d in (1, 2, 3)] + [((d, 0), 1) for d in (1, 2, 3)]

    def text_sem(slot, h):
        if (slot, h) in first_hop:
            return txt_r.at[first_hop.index((slot, h))]
        return txt_r.at[6 + TSLOT[slot] // 4]

    def send_text(source, h, dy, dx):
        landing = ((source[0] - dy) % 4, (source[1] - dx) % 4)
        copy(
            txt.at[TSLOT[source], rows(h)], txt.at[TSLOT[landing], rows(h)],
            sent.at[TXT], text_sem(landing, h), at_plane(dy, dx),
        ).start()

    def image_sem(d, h):
        return img_r.at[{2: h, 6: 2 + h, 1: 4, 7: 5, 3: 6, 5: 7, 4: 8}[d]]

    def send_image(source, h, d):
        landing = (source - d) % 8
        copy(
            img.at[ISLOT[0, source], rows(h)], img.at[ISLOT[0, landing], rows(h)],
            sent.at[IMG], image_sem(landing, h), at_line(0, d),
        ).start()

    def send_pair(d):
        if d in (1, 7, 3, 5, 4):
            take(img.at[ISLOT[0, d]], image_sem(d, 0))
        copy(
            img.at[ISLOT[0, d]], img.at[ISLOT[1, d]],
            sent.at[PAIR], pair_r.at[int(d in FAR)], at_line(1, 0),
        ).start()

    def spread(source, h):
        if (source, h) in first_hop:
            take(txt.at[TSLOT[source], rows(h)], text_sem(source, h))
        for d in ROUND:
            send_text(source, h, *((d, 0) if h == 0 else (0, d)))

    def relay(source, h):
        take(img.at[ISLOT[0, source], rows(h)], image_sem(source, h))
        if source == 6:
            if h == 0:
                send_image(6, 0, 2)
            send_image(6, h, 1)
        else:
            if h == 1:
                send_image(2, 1, 6)
            send_image(2, h, 7)

    send_image(0, 0, 2)
    send_image(0, 0, 6)
    send_image(0, 1, 2)
    send_image(0, 1, 6)
    for d in (1, 3, 2):
        send_text((0, 0), 0, 0, d)
        send_text((0, 0), 1, d, 0)
    for h in range(2):
        send_image(0, h, 1)
        send_image(0, h, 7)
    spread((0, 0), 0)
    spread((0, 0), 1)
    send_pair(0)
    relay(6, 0)
    relay(2, 0)
    for d in (3, 1):
        spread((0, d), 0)
        spread((d, 0), 1)
    relay(6, 1)
    relay(2, 1)
    spread((0, 2), 0)
    spread((2, 0), 1)
    for d in (2, 6, 1, 7):
        send_pair(d)

    power = scale * (0.5 * math.log2(math.e))
    down, up = math.exp(-15.0), math.exp(15.0)

    def strips(first, last, g):
        c = pl.multiple_of(g * 256, 256)
        right = txt[pl.ds(4 * g, 4)].reshape(256, 512)
        hi_col = col_hi[:, pl.ds(c, 256)]
        lo_col = col_lo[:, pl.ds(c, 256)]
        for i in range(first, last):
            r = 128 * i
            left = img[2 * i : 2 * i + 2].reshape(128, 512)
            dots = lax.dot_general(left, right, NT, preferred_element_type=f32)
            f = jnp.exp2(dots * power)
            half[r : r + 128, pl.ds(c, 256)] = f
            hi = f * down
            hi = hi * hi
            lo = jnp.minimum(f, 1.0) * up
            lo = lo * lo
            row_part[0, r : r + 128, :] += hi[:, :128] + hi[:, 128:]
            row_part[1, r : r + 128, :] += lo[:, :128] + lo[:, 128:]
            hi_col = hi_col + jnp.sum(hi.reshape(16, 8, 256), axis=0)
            lo_col = lo_col + jnp.sum(lo.reshape(16, 8, 256), axis=0)
        col_hi[:, pl.ds(c, 256)] = hi_col
        col_lo[:, pl.ds(c, 256)] = lo_col

    def need_group(g):
        count = 8 - sum(TSLOT[slot] // 4 == g for slot, _ in first_hop) - 2 * (g == 0)
        take(img.at[pl.ds(0, count), rows(0)], txt_r.at[6 + g])

    take(img.at[pl.ds(0, 5)], pair_r.at[0])
    need_group(0)
    strips(0, 5, 0)
    need_group(1)
    strips(0, 5, 1)
    need_group(2)
    strips(0, 5, 2)
    for d in FAR:
        send_pair(d)
    need_group(3)
    strips(0, 5, 3)

    @pl.loop(0, 4)
    def _(g):
        strips(5, 6, g)

    take(img.at[pl.ds(0, 3)], pair_r.at[1])

    @pl.loop(0, 4)
    def _(g):
        strips(6, 8, g)

    def log_of(hi, lo):
        return jnp.where(
            hi >= math.exp(-30.0), jnp.log(hi) + 30.0, jnp.log(lo) - 30.0
        )

    row_hi = jnp.sum(row_part[0].T, axis=0, keepdims=True)
    row_lo = jnp.sum(row_part[1].T, axis=0, keepdims=True)
    row_stat[0, :, :1024] = log_of(row_hi, row_lo)
    same = img[0].astype(f32) * txt[0].astype(f32)
    positive = scale * jnp.sum(same)
    row_stat[0, :, 1024:] = jnp.full((1, 128), positive, f32)
    for d in (4, 3, 5, 2, 6, 1, 7, 0):
        for k in range(2):
            if k or d:
                b = ISLOT[k, (8 - d) % 8]
                copy(row_stat.at[0], row_stat.at[b], sent.at[RSTAT], stat_r.at[0], at_line(k, d)).start()
    col_stat[0] = log_of(
        jnp.sum(col_hi[...], axis=0, keepdims=True), jnp.sum(col_lo[...], axis=0, keepdims=True)
    )
    for dy, dx in reversed(PLANE[1:]):
        b = TSLOT[(4 - dy) % 4, (4 - dx) % 4]
        copy(col_stat.at[0], col_stat.at[b], sent.at[CSTAT], stat_r.at[1], at_plane(dy, dx)).start()
    for j, raw in enumerate((raw_img, raw_txt)):
        unit[j], length = normal(raw)
        over_length[j] = jnp.broadcast_to(1.0 / length, (n, 128))
    take(row_stat.at[pl.ds(1, 15)], stat_r.at[0])
    take(col_stat.at[pl.ds(1, 15)], stat_r.at[1])

    def row_order(j):
        k, d = LINE[j]
        parts = row_stat[j, :, :1024]
        pieces = [None] * 16
        for p, (k2, d2) in enumerate(LINE):
            pieces[ISLOT[(k + k2) % 2, (d + d2) % 8]] = parts[:, p * n : p * n + n]
        return jnp.concatenate(pieces, axis=1)

    def col_order(j):
        dy, dx = PLANE[j]
        parts = col_stat[j]
        pieces = [None] * 16
        for p, (y2, x2) in enumerate(PLANE):
            pieces[TSLOT[(dy + y2) % 4, (dx + x2) % 4]] = parts[:, p * n : p * n + n]
        return jnp.concatenate(pieces, axis=1)

    def merged(parts):
        summit = functools.reduce(jnp.maximum, parts)
        total = sum(jnp.exp(p - summit) for p in parts)
        return summit + jnp.log(total)

    row_lse = merged([row_order(j) for j in range(16)])
    col_lse = merged([col_order(j) for j in range(16)])

    root = math.sqrt(0.5)
    row_factor = jnp.exp(row_lse * -0.5) * root
    col_factor = jnp.exp(col_lse * -0.5) * root
    row_scale[...] = jnp.broadcast_to(row_factor, (128, 1024)).T

    def weigh(first, last):
        for r in range(64 * first, 64 * last, 64):
            a = row_scale[r : r + 64, :]
            for q in range(0, 1024, 128):
                f = half[r : r + 64, q : q + 128]
                by_row = f * a
                by_col = f * col_factor[:, q : q + 128]
                weights[r : r + 64, q : q + 128] = (by_row * by_row + by_col * by_col).astype(bf16)

    texts = txt[...].reshape(1024, 512)
    images = img[...].reshape(1024, 512)

    def image_share(first, last):
        return jnp.dot(
            weights[first * n : last * n, :], texts, preferred_element_type=f32
        ).reshape(last - first, n, 512)

    def send_share(h, first, last, to):
        img_out[first:last] = image_share(first, last).astype(bf16)
        count = last - first
        copy(
            img_out.at[pl.ds(first, count)], img_pair.at[pl.ds(to, count)],
            sent.at[SHARE], pg_r.at[h], at_line(1, 0),
        ).start()

    def text_shares(g):
        part = lax.dot_general(
            weights[:, g * 256 : g * 256 + 256], images, TN, preferred_element_type=f32
        ).reshape(4, n, 512)
        txt_out[4 * g : 4 * g + 4] = part.astype(bf16)
        for slot in PLANE[4 * g : 4 * g + 4]:
            dy, dx = slot
            j = TSLOT[slot]
            if dy:
                b = TSLOT[(4 - dy) % 4, dx]
                copy(
                    txt_out.at[j, rows(0)], txt_mid.at[b, rows(0)],
                    sent.at[TMID], tm_r.at[2 * dx], at_plane(dy, 0),
                ).start()
            if dx:
                b = TSLOT[dy, (4 - dx) % 4]
                copy(
                    txt_out.at[j, rows(1)], txt_mid.at[b, rows(1)],
                    sent.at[TMID], tm_r.at[2 * dy + 1], at_plane(0, dx),
                ).start()

    def send_mid(j, slot, h, to):
        copy(
            img_out.at[slot, rows(h)], img_mid.at[j, rows(h)],
            sent.at[MID], im_r.at[h], at_line(0, to),
        ).start()

    weigh(13, 16)
    send_share(0, 13, 16, 5)
    all_positive = sum(row_stat[j, :, 1024:] for j in range(16))
    row_loss[0] = jnp.full((1, 128), jnp.sum(row_lse), f32) - 2.0 * all_positive
    col_loss[0] = jnp.full((1, 128), jnp.sum(col_lse), f32)
    for dy, dx in PLANE[1:]:
        b = TSLOT[(4 - dy) % 4, (4 - dx) % 4]
        copy(row_loss.at[0], row_loss.at[b], sent.at[RLOSS], stat_r.at[2], at_plane(dy, dx)).start()
    for k, d in LINE[1:]:
        b = ISLOT[k, (8 - d) % 8]
        copy(col_loss.at[0], col_loss.at[b], sent.at[CLOSS], stat_r.at[3], at_line(k, d)).start()
    weigh(10, 13)
    weigh(5, 10)
    send_share(1, 5, 10, 0)
    weigh(0, 5)
    text_shares(3)
    text_shares(2)
    part = image_share(10, 13)
    take(img_pair.at[pl.ds(5, 3)], pg_r.at[0])
    img_out[10:13] = (part + img_pair[5:8].astype(f32)).astype(bf16)
    for h in range(2):
        send_mid(0, 10, h, 1)
        send_mid(1, 11, h, 7)
        send_mid(2, 12, h, (2, 6)[h])
    text_shares(1)
    text_shares(0)
    part = image_share(0, 5)
    take(img_pair.at[pl.ds(0, 5)], pg_r.at[1])
    part = part + img_pair[0:5].astype(f32)
    img_own[...] = part[0]
    img_hold[...] = part[1:3]
    img_out[3:5] = part[3:5].astype(bf16)
    for j, d in ((0, 1), (1, 7)):
        copy(img_out.at[3 + j], img_in.at[j], sent.at[LAST], ig_r.at[0], at_line(0, d)).start()

    def mid(j, h):
        return img_mid[j, 32 * h : 32 * h + 32, :].astype(f32)

    for h in range(2):
        take(img_mid.at[pl.ds(0, 3), rows(h)], im_r.at[h])
        for j, d in ((0, 2), (1, 6)):
            total = img_hold[j, 32 * h : 32 * h + 32, :] + mid(j, h)
            if h == j:
                total = total + mid(2, h)
            img_send[j, 32 * h : 32 * h + 32, :] = total.astype(bf16)
            copy(
                img_send.at[j, rows(h)], img_in.at[2 + j, rows(h)],
                sent.at[LAST], ig_r.at[0], at_line(0, d),
            ).start()

    def text_sum(d, h):
        slots = [(e, d) if h == 0 else (d, e) for e in range(4)]
        take(txt_mid.at[pl.ds(0, 3), rows(h)], tm_r.at[2 * d + h])
        total = txt_out[TSLOT[slots[0]], 32 * h : 32 * h + 32, :].astype(f32)
        for slot in slots[1:]:
            total = total + txt_mid[TSLOT[slot], 32 * h : 32 * h + 32, :].astype(f32)
        return total

    for d in ROUND:
        for h in range(2):
            txt_send[d, 32 * h : 32 * h + 32, :] = text_sum(d, h).astype(bf16)
            copy(
                txt_send.at[d, rows(h)], txt_in.at[4 - d, rows(h)],
                sent.at[END], tg_r.at[0], at_plane(*((0, d) if h == 0 else (d, 0))),
            ).start()
    txt_total = jnp.concatenate([text_sum(0, 0), text_sum(0, 1)], axis=0)

    def finish(j, total, other):
        gradient = scale * total - scale * other.astype(f32)
        inner = jnp.sum(unit[j] * gradient, axis=1, keepdims=True)
        return (gradient - unit[j] * inner) * over_length[j, :, :1]

    take(row_loss.at[pl.ds(1, 15)], stat_r.at[2])
    take(col_loss.at[pl.ds(1, 15)], stat_r.at[3])
    total = sum(row_loss[j] + col_loss[j] for j in range(16))
    loss_ref[...] = total / (2.0 * batch)
    take(img_in, ig_r.at[0])
    img_total = img_own[...]
    for j in range(4):
        img_total = img_total + img_in[j].astype(f32)
    img_grad_ref[...] = finish(0, img_total, txt[0])
    take(txt_in.at[pl.ds(1, 3)], tg_r.at[0])
    for d in range(1, 4):
        txt_total = txt_total + txt_in[d].astype(f32)
    txt_grad_ref[...] = finish(1, txt_total, img[0])
    drain(txt.at[pl.ds(0, 15)], TXT)
    drain(img.at[pl.ds(0, 7)], IMG)
    drain(img.at[pl.ds(0, 8)], PAIR)
    drain(row_stat.at[pl.ds(1, 15)], RSTAT)
    drain(col_stat.at[pl.ds(1, 15)], CSTAT)
    drain(row_loss.at[pl.ds(1, 15)], RLOSS)
    drain(col_loss.at[pl.ds(1, 15)], CLOSS)
    drain(img_pair, SHARE)
    drain(img_mid, MID)
    drain(img_in, LAST)
    drain(txt.at[pl.ds(0, 12)], TMID)
    drain(txt_in.at[pl.ds(1, 3)], END)


def write_out(loss_in, img_in, txt_in, loss_out, img_out, txt_out):
    loss_out[...] = loss_in[0, :1]
    img_out[...] = img_in[...]
    txt_out[...] = txt_in[...]


def on_device(image, text, logit_scale):
    batch = image.shape[0] * 256
    f32, bf16 = jnp.float32, jnp.bfloat16
    dma = pltpu.SemaphoreType.DMA
    vmem = pltpu.VMEM
    hbm = pl.BlockSpec(memory_space=pltpu.HBM)
    local = pl.BlockSpec(memory_space=vmem)
    loss, img_grad, txt_grad = pl.pallas_call(
        functools.partial(kernel, batch),
        out_shape=(
            jax.ShapeDtypeStruct((1, 128), f32),
            jax.ShapeDtypeStruct((64, 512), f32),
            jax.ShapeDtypeStruct((64, 512), f32),
        ),
        in_specs=[hbm, hbm, hbm],
        out_specs=[local] * 3,
        scratch_shapes=[
            vmem((64, 512), bf16),
            vmem((64, 512), bf16),
            pltpu.SMEM((1,), f32),
            vmem((2, 64, 512), f32),
            vmem((2, 64, 128), f32),
            vmem((16, 64, 512), bf16),
            vmem((16, 64, 512), bf16),
            vmem((1024, 1024), f32),
            vmem((1024, 1024), bf16),
            vmem((2, 1024, 128), f32),
            vmem((1024, 128), f32),
            vmem((8, 1024), f32),
            vmem((8, 1024), f32),
            vmem((16, 1, 1152), f32),
            vmem((16, 1, 1024), f32),
            vmem((16, 1, 128), f32),
            vmem((16, 1, 128), f32),
            vmem((16, 64, 512), bf16),
            vmem((8, 64, 512), bf16),
            vmem((2, 64, 512), f32),
            vmem((3, 64, 512), bf16),
            vmem((2, 64, 512), bf16),
            vmem((4, 64, 512), bf16),
            vmem((64, 512), f32),
            vmem((16, 64, 512), bf16),
            vmem((16, 64, 512), bf16),
            vmem((4, 64, 512), bf16),
            vmem((4, 64, 512), bf16),
            dma((3,)), dma((12,)), dma((10,)), dma((9,)), dma((2,)), dma((4,)), dma((2,)), dma((2,)),
            dma((1,)), dma((8,)), dma((1,)),
        ],
        compiler_params=pltpu.CompilerParams(
            collective_id=0, has_side_effects=True, vmem_limit_bytes=56 * 2**20
        ),
        cost_estimate=pl.CostEstimate(
            flops=6 * 1024 * 1024 * 512, bytes_accessed=400000, transcendentals=1024 * 1024
        ),
        name="contrast",
    )(image, text, logit_scale)
    return pl.pallas_call(
        write_out,
        out_shape=(
            jax.ShapeDtypeStruct((1,), f32),
            jax.ShapeDtypeStruct((64, 512), f32),
            jax.ShapeDtypeStruct((64, 512), f32),
        ),
        in_specs=[local] * 3,
        out_specs=[local] * 3,
        name="write_out",
    )(loss, img_grad, txt_grad)


def solution(mesh):
    torus = Mesh(mesh.devices.reshape(8, 4, 4, 2), AXES)
    return jax.shard_map(
        on_device,
        mesh=torus,
        in_specs=(P(AXES, None), P(AXES, None), P()),
        out_specs=(P(), P(AXES, None), P(AXES, None)),
        check_vma=False,
    )
```
